32 devices in a mesh: parts: 2 (over x), owner: 16 (over z, y, core).
Axes of the slice: x: 2, y: 2, z: 4, core: 2. Of those that a mesh axis runs over, the one named last changes fastest.
Arguments:
- embeddings: bfloat16 [131072, 768], P(('parts', 'owner')), parts along dimension 0, may hold values from -6 to 6
- cluster_ids: int32 [131072], P(('parts', 'owner')), parts along dimension 0, may hold values from 0 to 63, as said below
- member_ranks: int32 [131072], P(('parts', 'owner')), parts along dimension 0, may hold values from 0 to 2047, as said below
Outputs:
- max_similarity: float32 [131072], P(('parts', 'owner')), parts along dimension 0
The draws below stay inside these ranges and needn't reach their ends.
There are 2 independent parts, one for each index of `parts`. The reference program is written for one: setup_inputs(seed, part) draws one part's arguments, and reference() takes and returns one part's arrays. A program takes and returns all parts, laid end to end along the dimension named above; each array names one. Nothing has to cross between parts.
Inputs may be any that keep to these rules, and one draw needn't show every extreme that they name: `cluster_ids`: A cluster holds at most 2048 rows, and some cluster holds exactly 2048. At most 128 rows of one device belong to one cluster, reached on every device. For every o, the rows of one device with ids from 4 * o to 4 * o + 3 number at most 512, reached on every device. For every k, the rows of one device with ids from 2 * 4 * k to 2 * 4 * k + 2 * 4 - 1 number at most 512, reached on every device. `member_ranks`: within each cluster of s rows the ranks of its rows are 0 to s - 1, each once.
All inputs are finite; a program needn't handle non-finite values.
Results may differ from the reference program's by a relative error of at most 0.0003.
Values may be sent and summed in bfloat16 or wider, within the bound.
No kernel may reach another device: no remote copies, remote signals or barrier semaphores. Data moves between devices by JAX's collectives and lax.ppermute only.
A program may use at most 128 MiB of HBM per device.

```python
import jax
import jax.numpy as jnp
from jax import lax

D = 768
ROWS_DEV = 4096
CL_DEV = 4
CMAX = 2048
CAP = 512
NCLUST = 64
ROWS = 65536
N_OWNER = 16


def layout(key):
    key_heavy, key_split, key_offset, key_shuffle, key_order = jax.random.split(key, 5)
    owners = N_OWNER
    pair_count = owners // 2
    heavy_owner = jax.random.randint(key_heavy, (), 0, owners)
    shares = jax.random.randint(key_split, (owners, pair_count), 0, CAP + 1)
    counts = jnp.stack([shares, CAP - shares], -1).reshape(owners, owners)
    owner_list = jnp.arange(owners, dtype=jnp.int32)
    forced = jnp.where(owner_list == heavy_owner, CAP, 0)
    counts = jnp.where((owner_list // 2)[None, :] == heavy_owner // 2, forced[None, :], counts)
    bucket_end = jnp.cumsum(counts, 1)
    bucket_start = bucket_end - counts
    position_list = jnp.arange(ROWS_DEV, dtype=jnp.int32)
    destination = jnp.sum((position_list[None, :, None] >= bucket_end[:, None, :]).astype(jnp.int32), -1)
    within = position_list[None, :] - jnp.take_along_axis(bucket_start, destination, 1)
    offset = jax.random.randint(key_offset, (owners, owners), 0, CL_DEV)
    shift_pick = jnp.take_along_axis(offset, destination, 1)
    slot_pick = (within // (CAP // CL_DEV) + shift_pick) % CL_DEV
    sorted_ids = destination * CL_DEV + slot_pick
    device_keys = jax.random.split(key_shuffle, owners)
    shuffles = jax.vmap(lambda device_key: jax.random.permutation(device_key, ROWS_DEV))(device_keys)
    cluster_ids = jnp.take_along_axis(sorted_ids, shuffles, 1).reshape(-1).astype(jnp.int32)
    tiebreak = jax.random.permutation(key_order, ROWS).astype(jnp.int32)
    sort_score = cluster_ids * ROWS + tiebreak
    sort_order = jnp.argsort(sort_score, stable=True)
    position = jnp.zeros((ROWS,), jnp.int32).at[sort_order].set(jnp.arange(ROWS, dtype=jnp.int32))
    cluster_size = jnp.zeros((NCLUST,), jnp.int32).at[cluster_ids].add(1)
    first_rank = jnp.cumsum(cluster_size) - cluster_size
    member_ranks = (position - first_rank[cluster_ids]).astype(jnp.int32)
    return (cluster_ids, member_ranks)


def draw_cluster_ids(key, part):
    cluster_ids, member_ranks = layout(key)
    return cluster_ids


def draw_member_ranks(key, part):
    cluster_ids, member_ranks = layout(key)
    return member_ranks


def block_levels(rng, shape, shards, smallest, high):
    def one(dim, parts):
        steps = jax.random.uniform(jax.random.fold_in(jax.random.fold_in(rng, 6), dim), (parts,), jnp.float32, smallest / len(shards), high / len(shards))
        return jnp.repeat(jnp.exp(steps), shape[dim] // parts).reshape((-1,) + (1,) * (len(shape) - dim - 1))

    gain = one(*shards[0])
    for cut in shards[1:]:
        gain = gain * one(*cut)
    return gain


def noise(key, dims, deviation, limit, pieces=(), kind=jnp.bfloat16):
    values = deviation * jax.random.normal(key, dims, jnp.float32)
    if pieces:
        values = values * block_levels(key, dims, pieces, -0.22, 0.18)
    return jnp.clip(values, -limit, limit).astype(kind)


def setup_inputs(seed: int = 0, part: int = 0) -> dict:
    key_list = jax.random.split(jax.random.key(seed), 4)
    part_splits = jax.random.split(jax.random.fold_in(key_list[3], part), 4)
    return {
        "embeddings": noise(part_splits[0], (ROWS, D), 1.0, 6.0, ((0, 16),)),
        "cluster_ids": draw_cluster_ids(jax.random.fold_in(jax.random.fold_in(key_list[3], part), 71), part),
        "member_ranks": draw_member_ranks(jax.random.fold_in(jax.random.fold_in(key_list[3], part), 71), part),
    }


epsilon = 1e-06

def reference(embeddings, cluster_ids, member_ranks):
    position = (cluster_ids * CMAX + member_ranks).astype(jnp.int32)
    squares = lax.optimization_barrier(jnp.sum(jnp.square(embeddings.astype(jnp.float32)), 1))
    inverse = lax.rsqrt(squares + epsilon)
    buffer_rows = jnp.zeros((NCLUST * CMAX, D), embeddings.dtype).at[position].set(embeddings)
    inverse_rows = jnp.zeros((NCLUST * CMAX,), jnp.float32).at[position].set(inverse)
    index_list = jnp.arange(CMAX, dtype=jnp.int32)
    earlier = index_list[None, :] < index_list[:, None]

    def one_cluster(cluster):
        start = (cluster * CMAX).astype(jnp.int32)
        members = lax.dynamic_slice_in_dim(buffer_rows, start, CMAX, 0)
        member_inv = lax.dynamic_slice_in_dim(inverse_rows, start, CMAX, 0)
        scores = lax.dot_general(members, members, (((1,), (1,)), ((), ())), preferred_element_type=jnp.float32)
        scores = scores * member_inv[:, None] * member_inv[None, :]
        return lax.optimization_barrier(jnp.max(jnp.where(earlier, scores, -1.0), 1))
    best_sim = lax.map(one_cluster, jnp.arange(NCLUST, dtype=jnp.int32)).reshape(-1)
    return best_sim[position]
```

```python
import functools

import jax
import jax.numpy as jnp
from jax import lax
from jax.experimental import pallas as pl
from jax.experimental.pallas import tpu as pltpu
from jax.sharding import PartitionSpec as P

CL_DEV = 4
CMAX = 2048
EPSILON = 1e-06
MASKED = -30000.0
GROUP = 2 * CL_DEV
LANES = 128
VMEM_LIMIT = 48 * 1024 * 1024


def params():
    return pltpu.CompilerParams(vmem_limit_bytes=VMEM_LIMIT)


def nt_dot(a, b):
    return lax.dot_general(a, b, (((1,), (1,)), ((), ())), preferred_element_type=jnp.float32)


def one_hot(condition):
    return jnp.where(condition, 1.0, 0.0).astype(jnp.bfloat16)


def tile_lanes(x, times):
    return jnp.concatenate([x] * times, 1)


def order_kernel(block_rows, ids_ref, ranks_ref, pos_ref, keys_ref, local_ref):
    rows = ids_ref.shape[1]
    clusters = local_ref.shape[0]
    chunk = 256
    cluster_iota = lax.broadcasted_iota(jnp.int32, (clusters, chunk), 0)
    before = one_hot(
        lax.broadcasted_iota(jnp.int32, (chunk, chunk), 0)
        < lax.broadcasted_iota(jnp.int32, (chunk, chunk), 1)
    )
    ones = jnp.ones((chunk, LANES), jnp.bfloat16)
    count = jnp.zeros((clusters, LANES), jnp.float32)
    for start in range(0, rows, chunk):
        hot = one_hot(ids_ref[:, start : start + chunk] == cluster_iota)
        prefix = jnp.dot(hot, before, preferred_element_type=jnp.float32)
        local_ref[:, start : start + chunk] = prefix + tile_lanes(count, chunk // LANES)
        count += jnp.dot(hot, ones, preferred_element_type=jnp.float32)
    lower = one_hot(
        lax.broadcasted_iota(jnp.int32, (clusters, clusters), 1)
        < lax.broadcasted_iota(jnp.int32, (clusters, clusters), 0)
    )
    offset = jnp.dot(lower, count.astype(jnp.bfloat16), preferred_element_type=jnp.float32)
    offset = tile_lanes(offset, chunk // LANES)
    high_rows = rows // LANES
    table = jnp.zeros((2 * high_rows, LANES), jnp.float32)
    high_iota = lax.broadcasted_iota(jnp.int32, (high_rows, chunk), 0)
    low_iota = lax.broadcasted_iota(jnp.int32, (LANES, chunk), 0)
    for start in range(0, rows, chunk):
        ids = ids_ref[:, start : start + chunk]
        place = jnp.where(
            ids == cluster_iota, local_ref[:, start : start + chunk] + offset, 0.0
        )
        position = jnp.sum(place, 0, keepdims=True).astype(jnp.int32)
        pos_ref[:, start : start + chunk] = position
        key = (ids & (GROUP - 1)) * CMAX + ranks_ref[:, start : start + chunk]
        high_hot = (position >> 7) == high_iota
        key_high = (key >> 7).astype(jnp.float32)
        key_low = (key & 127).astype(jnp.float32)
        left = jnp.concatenate(
            [jnp.where(high_hot, key_high, 0.0), jnp.where(high_hot, key_low, 0.0)], 0
        ).astype(jnp.bfloat16)
        table += nt_dot(left, one_hot((position & 127) == low_iota))
    keys = (table[:high_rows] * 128.0 + table[high_rows:]).astype(jnp.int32)
    per_block = block_rows // LANES
    for group in range(rows // block_rows):
        piece = keys[group * per_block : (group + 1) * per_block]
        keys_ref[2 * group] = piece
        keys_ref[2 * group + 1] = piece


def order_rows(ids, ranks, chips, block_rows):
    rows = ids.shape[0]
    return pl.pallas_call(
        functools.partial(order_kernel, block_rows),
        out_shape=(
            jax.ShapeDtypeStruct((1, rows), jnp.int32),
            jax.ShapeDtypeStruct((2 * chips, block_rows // LANES, LANES), jnp.int32),
        ),
        scratch_shapes=[pltpu.VMEM((chips * GROUP, rows), jnp.float32)],
        compiler_params=params(),
        cost_estimate=pl.CostEstimate(flops=10**9, bytes_accessed=10**5, transcendentals=0),
        name="order_rows",
    )(ids.reshape(1, rows), ranks.reshape(1, rows))


def pick_kernel(group_ref, pos_ref, rows_ref, out_ref, total):
    step = pl.program_id(0)
    block_rows, depth = out_ref.shape[0], rows_ref.shape[0]
    target = lax.broadcasted_iota(jnp.int32, (block_rows, depth), 0) + group_ref[0] * block_rows
    part = jnp.dot(one_hot(pos_ref[...] == target), rows_ref[...], preferred_element_type=jnp.float32)

    @pl.when(step == 0)
    def _():
        total[...] = part

    @pl.when(step > 0)
    def _():
        total[...] += part

    @pl.when(step == pl.num_programs(0) - 1)
    def _():
        out_ref[...] = total[...].astype(out_ref.dtype)


def pick_block(group, position, embeddings, block_rows):
    rows, width = embeddings.shape
    depth = 1024
    return pl.pallas_call(
        pick_kernel,
        grid_spec=pltpu.PrefetchScalarGridSpec(
            num_scalar_prefetch=1,
            grid=(rows // depth,),
            in_specs=[
                pl.BlockSpec((1, depth), lambda i, g: (0, i)),
                pl.BlockSpec((depth, width), lambda i, g: (i, 0)),
            ],
            out_specs=pl.BlockSpec((block_rows, width), lambda i, g: (0, 0)),
            scratch_shapes=[pltpu.VMEM((block_rows, width), jnp.float32)],
        ),
        out_shape=jax.ShapeDtypeStruct((block_rows, width), embeddings.dtype),
        compiler_params=params(),
        cost_estimate=pl.CostEstimate(
            flops=2 * block_rows * rows * width, bytes_accessed=2 * rows * width, transcendentals=0
        ),
        name="pick_block",
    )(group, position, embeddings)


def inverse_kernel(rows_ref, out_ref):
    count = rows_ref.shape[0]
    for start in range(0, count, LANES):
        x = rows_ref[start : start + LANES].astype(jnp.float32)
        inverse = lax.rsqrt(jnp.sum(x * x, 1, keepdims=True) + EPSILON)
        spread = jnp.transpose(jnp.broadcast_to(inverse, (LANES, LANES)))
        out_ref[:, start : start + LANES] = spread[0:1]


def inverse_norms(embeddings):
    rows, width = embeddings.shape
    block = 512
    return pl.pallas_call(
        inverse_kernel,
        grid=(rows // block,),
        in_specs=[pl.BlockSpec((block, width), lambda i: (i, 0))],
        out_specs=pl.BlockSpec((1, block), lambda i: (0, i)),
        out_shape=jax.ShapeDtypeStruct((1, rows), jnp.float32),
        compiler_params=params(),
        cost_estimate=pl.CostEstimate(
            flops=4 * rows * width, bytes_accessed=2 * rows * width, transcendentals=0
        ),
        name="inverse_norms",
    )(embeddings)


def lane_keys(keys_ref, index):
    keys = keys_ref[index]
    return jnp.concatenate([keys[i : i + 1] for i in range(keys.shape[0])], 1)


def best_of(columns, column_inverse, column_key, queries, query_key):
    count = queries.shape[0]
    scores = nt_dot(columns, queries)
    scores = scores * tile_lanes(column_inverse, count // LANES)
    rank = query_key & (CMAX - 1)
    base = query_key - rank
    earlier = (tile_lanes(column_key, count // LANES) ^ base) < rank
    scores = jnp.where(earlier, scores, MASKED)
    return jnp.max(scores.reshape(scores.shape[0] // 8, 8, count), 0)


def step_kernel(old, slot_ref, keys_ref, own_ref, other_ref, *refs):
    if old:
        (rows_ref, inverse_ref, spread_ref, best_in, rows_out, inverse_out, spread_out, best_out,
         running) = refs
    else:
        rows_out, inverse_out, spread_out, best_out, running = refs
    block = own_ref.shape[0]
    step = pl.program_id(0)
    tile = 256
    own_key = lane_keys(keys_ref, slot_ref[old, 0])

    @pl.when(step == 0)
    def _():
        for side, ref in ((0, own_ref), (1, other_ref)):
            rows_out[0, side] = ref[...]
            keys = keys_ref[slot_ref[old, side]]
            for start in range(0, block, LANES):
                x = ref[start : start + LANES].astype(jnp.float32)
                inverse = lax.rsqrt(jnp.sum(x * x, 1, keepdims=True) + EPSILON)
                inverse_out[0, side, start : start + LANES] = jnp.broadcast_to(inverse, (LANES, LANES))
                piece = start // LANES
                spread_out[0, side, start : start + LANES] = jnp.transpose(
                    jnp.broadcast_to(keys[piece : piece + 1], (LANES, LANES))
                )
        running[...] = jnp.full(running.shape, MASKED, jnp.float32)

    if old:

        @pl.when(step < old)
        def _():
            old_key = lane_keys(keys_ref, slot_ref[step, 0])
            old_best = best_in[0]
            new_best = running[...]
            for side, ref in ((0, own_ref), (1, other_ref)):
                for start in range(0, block, tile):
                    cut = slice(start, start + tile)
                    old_best = jnp.maximum(
                        old_best,
                        best_of(ref[cut], inverse_out[0, side, cut], spread_out[0, side, cut],
                                rows_ref[0, 0], old_key),
                    )
                    new_best = jnp.maximum(
                        new_best,
                        best_of(rows_ref[0, side, cut], inverse_ref[0, side, cut],
                                spread_ref[0, side, cut], own_ref[...], own_key),
                    )
            best_out[0] = old_best
            running[...] = new_best

    @pl.when(step == old)
    def _():
        new_best = running[...]
        for side, ref in ((0, own_ref), (1, other_ref)):
            for start in range(0, block, tile):
                cut = slice(start, start + tile)
                new_best = jnp.maximum(
                    new_best,
                    best_of(ref[cut], inverse_out[0, side, cut], spread_out[0, side, cut],
                            own_ref[...], own_key),
                )
        best_out[0] = new_best


def match_step(old, chips, slots, keys, own, other, state):
    block, width = own.shape

    def whole(shape):
        return pl.BlockSpec(shape, lambda i, s: (0,) * len(shape))

    def old_block(shape):
        return pl.BlockSpec(
            (1,) + shape, lambda i, s: (jnp.minimum(i, old - 1),) + (0,) * len(shape)
        )

    def new_block(shape):
        return pl.BlockSpec((1,) + shape, lambda i, s: (old,) + (0,) * len(shape))

    in_specs = [whole(keys.shape), whole((block, width)), whole((block, width))]
    if old:
        in_specs += [
            old_block((2, block, width)),
            old_block((2, block, LANES)),
            old_block((2, block, LANES)),
            old_block((8, block)),
        ]
    pairs = 2 * (2 * old + 1) * block * block
    return pl.pallas_call(
        functools.partial(step_kernel, old),
        grid_spec=pltpu.PrefetchScalarGridSpec(
            num_scalar_prefetch=1,
            grid=(old + 1,),
            in_specs=in_specs,
            out_specs=(
                new_block((2, block, width)),
                new_block((2, block, LANES)),
                new_block((2, block, LANES)),
                pl.BlockSpec((1, 8, block), lambda i, s: (i, 0, 0)),
            ),
            scratch_shapes=[pltpu.VMEM((8, block), jnp.float32)],
        ),
        out_shape=(
            jax.ShapeDtypeStruct((chips, 2, block, width), own.dtype),
            jax.ShapeDtypeStruct((chips, 2, block, LANES), jnp.float32),
            jax.ShapeDtypeStruct((chips, 2, block, LANES), jnp.int32),
            jax.ShapeDtypeStruct((chips, 8, block), jnp.float32),
        ),
        input_output_aliases={4 + i: i for i in range(4)} if old else {},
        compiler_params=params(),
        cost_estimate=pl.CostEstimate(
            flops=2 * pairs * width, bytes_accessed=4 * (old + 1) * block * width, transcendentals=0
        ),
        name="match_step",
    )(slots, keys, own, other, *state)


def answer_kernel(chip_ref, block_rows, table_ref, pos_ref, inverse_ref, out_ref):
    rows = pos_ref.shape[1]
    chunk = 512
    table = table_ref[...]
    high = table.astype(jnp.bfloat16)
    rest = table - high.astype(jnp.float32)
    middle = rest.astype(jnp.bfloat16)
    low = (rest - middle.astype(jnp.float32)).astype(jnp.bfloat16)
    high_iota = lax.broadcasted_iota(jnp.int32, (rows // LANES, chunk), 0)
    low_iota = lax.broadcasted_iota(jnp.int32, (LANES, chunk), 0)
    for start in range(0, rows, chunk):
        position = pos_ref[:, start : start + chunk] ^ (chip_ref[0] * block_rows)
        hot = one_hot((position >> 7) == high_iota)
        values = sum(
            lax.dot_general(part, hot, (((0,), (0,)), ((), ())), preferred_element_type=jnp.float32)
            for part in (high, middle, low)
        )
        best = jnp.sum(
            jnp.where((position & 127) == low_iota, values, 0.0), 0, keepdims=True
        )
        out_ref[:, start : start + chunk] = jnp.maximum(
            best * inverse_ref[:, start : start + chunk], -1.0
        )


def answer_rows(chip, table, position, inverse, block_rows):
    rows = position.shape[1]

    def body(chip_ref, *refs):
        answer_kernel(chip_ref, block_rows, *refs)

    return pl.pallas_call(
        body,
        in_specs=[pl.BlockSpec(memory_space=pltpu.SMEM)] + [pl.BlockSpec(memory_space=pltpu.VMEM)] * 3,
        out_shape=jax.ShapeDtypeStruct((1, rows), jnp.float32),
        compiler_params=params(),
        name="answer_rows",
    )(chip, table, position, inverse)


def on_device(embeddings, cluster_ids, member_ranks):
    rows, width = embeddings.shape
    owners = lax.axis_size("owner")
    chips = owners // 2
    block = rows // chips
    me = lax.axis_index("owner").astype(jnp.int32)
    chip, core = me // 2, me % 2

    def across(x, d):
        return lax.ppermute(x, "owner", [(i, i ^ (2 * d)) for i in range(owners)])

    def swap(x):
        return lax.ppermute(x, "owner", [(i, i ^ 1) for i in range(owners)])

    position, send_keys = order_rows(cluster_ids, member_ranks, chips, block)

    def pick(d):
        return pick_block((chip ^ d).reshape(1), position, embeddings, block)

    near = list(range(1, chips // 2))
    far = list(range(chips // 2, chips))
    sends = [far[0]]
    visits = [0]
    for a, b in zip(near, far[1:]):
        sends += [a, b]
    for a, b in zip(near, far):
        visits += [a, b]
    visits.append(far[-1])
    own = {d: across(pick(d), d) for d in sends}
    own[0] = pick(0)
    keys = lax.all_to_all(send_keys, "owner", split_axis=0, concat_axis=0, tiled=True)
    inverse = inverse_norms(embeddings)
    slots = jnp.stack(
        [jnp.stack([2 * (chip ^ d) + core, 2 * (chip ^ d) + 1 - core]) for d in visits]
    )
    state = ()
    for turn, d in enumerate(visits):
        state = match_step(turn, chips, slots, keys, own[d], swap(own[d]), state)
    best = jnp.max(state[3], 1)
    spots = {d: best[turn : turn + 1] for turn, d in enumerate(visits)}
    table = jnp.concatenate([spots[d] for d in range(chips)], 0)
    bit = 1
    while bit < chips:
        split = table.reshape(chips // (2 * bit), 2, bit, block)
        got = across(split[:, 1], bit)
        table = jnp.stack([split[:, 0], got], 1).reshape(chips, block)
        bit *= 2
    table = table.reshape(rows // LANES, LANES)
    answer = answer_rows(chip.reshape(1), table, position, inverse, block)
    return answer.reshape(rows)


def solution(mesh):
    in_specs = (P(("parts", "owner"), None), P(("parts", "owner")), P(("parts", "owner")))
    out_specs = P(("parts", "owner"))
    return jax.shard_map(
        on_device, mesh=mesh, in_specs=in_specs, out_specs=out_specs, check_vma=False
    )
```

```python
import functools

import jax
import jax.numpy as jnp
from jax import lax
from jax.experimental import pallas as pl
from jax.experimental.pallas import tpu as pltpu
from jax.sharding import PartitionSpec as P

CL_DEV = 4
CMAX = 2048
EPSILON = 1e-06
MASKED = -30000.0
GROUP = 2 * CL_DEV
LANES = 128
VMEM_LIMIT = 24 * 1024 * 1024
MATCH_LIMIT = 20 * 1024 * 1024


def params():
    return pltpu.CompilerParams(vmem_limit_bytes=VMEM_LIMIT)


def nt_dot(a, b):
    return lax.dot_general(a, b, (((1,), (1,)), ((), ())), preferred_element_type=jnp.float32)


def one_hot(condition):
    return jnp.where(condition, 1.0, 0.0).astype(jnp.bfloat16)


def tile_lanes(x, times):
    return jnp.concatenate([x] * times, 1)


def order_kernel(ids_ref, ranks_ref, pos_ref, keys_ref, local_ref):
    rows = ids_ref.shape[1]
    clusters = local_ref.shape[0]
    chunk = 256
    cluster_iota = lax.broadcasted_iota(jnp.int32, (clusters, chunk), 0)
    before = one_hot(
        lax.broadcasted_iota(jnp.int32, (chunk, chunk), 0)
        < lax.broadcasted_iota(jnp.int32, (chunk, chunk), 1)
    )
    ones = jnp.ones((chunk, LANES), jnp.bfloat16)
    count = jnp.zeros((clusters, LANES), jnp.float32)
    for start in range(0, rows, chunk):
        hot = one_hot(ids_ref[:, start : start + chunk] == cluster_iota)
        prefix = jnp.dot(hot, before, preferred_element_type=jnp.float32)
        local_ref[:, start : start + chunk] = prefix + tile_lanes(count, chunk // LANES)
        count += jnp.dot(hot, ones, preferred_element_type=jnp.float32)
    lower = one_hot(
        lax.broadcasted_iota(jnp.int32, (clusters, clusters), 1)
        < lax.broadcasted_iota(jnp.int32, (clusters, clusters), 0)
    )
    offset = jnp.dot(lower, count.astype(jnp.bfloat16), preferred_element_type=jnp.float32)
    offset = tile_lanes(offset, chunk // LANES)
    high_rows = rows // LANES
    table = jnp.zeros((2 * high_rows, LANES), jnp.float32)
    high_iota = lax.broadcasted_iota(jnp.int32, (high_rows, chunk), 0)
    low_iota = lax.broadcasted_iota(jnp.int32, (LANES, chunk), 0)
    for start in range(0, rows, chunk):
        ids = ids_ref[:, start : start + chunk]
        place = jnp.where(
            ids == cluster_iota, local_ref[:, start : start + chunk] + offset, 0.0
        )
        position = jnp.sum(place, 0, keepdims=True).astype(jnp.int32)
        pos_ref[:, start : start + chunk] = position
        key = (ids & (GROUP - 1)) * CMAX + ranks_ref[:, start : start + chunk]
        high_hot = (position >> 7) == high_iota
        key_high = (key >> 7).astype(jnp.float32)
        key_low = (key & 127).astype(jnp.float32)
        left = jnp.concatenate(
            [jnp.where(high_hot, key_high, 0.0), jnp.where(high_hot, key_low, 0.0)], 0
        ).astype(jnp.bfloat16)
        table += nt_dot(left, one_hot((position & 127) == low_iota))
    keys = (table[:high_rows] * 128.0 + table[high_rows:]).astype(jnp.int32)
    for row in range(high_rows):
        keys_ref[row] = jnp.broadcast_to(keys[row : row + 1], (8, LANES))


def order_rows(ids, ranks, clusters):
    rows = ids.shape[0]
    return pl.pallas_call(
        order_kernel,
        out_shape=(
            jax.ShapeDtypeStruct((1, rows), jnp.int32),
            jax.ShapeDtypeStruct((rows // LANES, 8, LANES), jnp.int32),
        ),
        scratch_shapes=[pltpu.VMEM((clusters, rows), jnp.float32)],
        compiler_params=params(),
        cost_estimate=pl.CostEstimate(flops=10**9, bytes_accessed=10**5, transcendentals=0),
        name="order_rows",
    )(ids.reshape(1, rows), ranks.reshape(1, rows))


def key_rows(keys_ref, row, count, width):
    upper = lax.broadcasted_iota(jnp.int32, (8, LANES), 0) == 0
    tiles = []
    for i in range(count):
        key = keys_ref[row + i]
        tiles.append(jnp.where(upper, key >> 7, key & 127).astype(jnp.float32))
    tiles += [jnp.zeros((8, LANES), jnp.float32)] * (width // LANES - count)
    return jnp.concatenate(tiles, 1).astype(jnp.bfloat16)


def inverse_lanes(x):
    x = x.astype(jnp.float32)
    inverse = lax.rsqrt(jnp.sum(x * x, 1, keepdims=True) + EPSILON)
    return jnp.transpose(jnp.broadcast_to(inverse, (LANES, LANES)))[0:1]


def first_kernel(start_ref, keys_ref, pos_ref, rows_ref, out_ref, total):
    step = pl.program_id(0)
    count, width = total.shape
    depth = rows_ref.shape[0]
    target = lax.broadcasted_iota(jnp.int32, (count, depth), 0) + start_ref[0]
    part = jnp.dot(one_hot(pos_ref[...] == target), rows_ref[...], preferred_element_type=jnp.float32)

    @pl.when(step == 0)
    def _():
        total[...] = part

    @pl.when(step > 0)
    def _():
        total[...] += part

    @pl.when(step == pl.num_programs(0) - 1)
    def _():
        out_ref[:count] = total[...].astype(out_ref.dtype)
        out_ref[count:] = key_rows(keys_ref, start_ref[0] // LANES, count // LANES, width)


def pick_first(start, keys, position, embeddings, count):
    rows, width = embeddings.shape
    depth = 1024
    return pl.pallas_call(
        first_kernel,
        grid_spec=pltpu.PrefetchScalarGridSpec(
            num_scalar_prefetch=1,
            grid=(rows // depth,),
            in_specs=[
                pl.BlockSpec(keys.shape, lambda i, g: (0, 0, 0)),
                pl.BlockSpec((1, depth), lambda i, g: (0, i)),
                pl.BlockSpec((depth, width), lambda i, g: (i, 0)),
            ],
            out_specs=pl.BlockSpec((count + 8, width), lambda i, g: (0, 0)),
            scratch_shapes=[pltpu.VMEM((count, width), jnp.float32)],
        ),
        out_shape=jax.ShapeDtypeStruct((count + 8, width), embeddings.dtype),
        compiler_params=params(),
        cost_estimate=pl.CostEstimate(
            flops=2 * count * rows * width, bytes_accessed=2 * rows * width, transcendentals=0
        ),
        name="pick_first",
    )(start, keys, position, embeddings)


def rest_kernel(counts, start_ref, keys_ref, pos_ref, rows_ref, *refs):
    outs, inverse_ref = refs[:-1], refs[-1]
    rows, width = rows_ref.shape
    for k, count in enumerate(counts):
        out_ref = outs[k]
        start = start_ref[k]
        tile = min(count, 256)

        def one_tile(i, carry, out_ref=out_ref, start=start, tile=tile):
            target = lax.broadcasted_iota(jnp.int32, (tile, rows), 0) + (start + i * tile)
            picked = jnp.dot(
                one_hot(pos_ref[...] == target), rows_ref[...], preferred_element_type=jnp.float32
            )
            out_ref[pl.ds(pl.multiple_of(i * tile, tile), tile)] = picked.astype(out_ref.dtype)
            return carry

        lax.fori_loop(0, count // tile, one_tile, 0)
        out_ref[count:] = key_rows(keys_ref, start // LANES, count // LANES, width)

    for at in range(0, rows, LANES):
        inverse_ref[:, at : at + LANES] = inverse_lanes(rows_ref[at : at + LANES])


def pick_rest(starts, keys, position, embeddings, counts):
    rows, width = embeddings.shape
    vmem = pl.BlockSpec(memory_space=pltpu.VMEM)
    return pl.pallas_call(
        functools.partial(rest_kernel, counts),
        in_specs=[pl.BlockSpec(memory_space=pltpu.SMEM), vmem, vmem, vmem],
        out_shape=tuple(jax.ShapeDtypeStruct((count + 8, width), embeddings.dtype) for count in counts)
        + (jax.ShapeDtypeStruct((1, rows), jnp.float32),),
        out_specs=(vmem,) * (len(counts) + 1),
        compiler_params=params(),
        cost_estimate=pl.CostEstimate(
            flops=2 * sum(counts) * rows * width, bytes_accessed=4 * rows * width, transcendentals=0
        ),
        name="pick_rest",
    )(starts, keys, position, embeddings)


def new_keys(ref, count):
    parts = ref[count : count + 8, :count].astype(jnp.float32)
    return (parts[0:1] * 128.0 + parts[1:2]).astype(jnp.int32)


def best_of(columns, column_inverse, column_key, queries, query_key):
    count = queries.shape[0]
    scores = nt_dot(columns, queries)
    scores = scores * tile_lanes(column_inverse, count // LANES)
    rank = query_key & (CMAX - 1)
    base = query_key - rank
    earlier = (tile_lanes(column_key, count // LANES) ^ base) < rank
    scores = jnp.where(earlier, scores, MASKED)
    return jnp.max(scores.reshape(scores.shape[0] // 8, 8, count), 0)


def joined(ref, first, last):
    return jnp.concatenate([ref[i] for i in range(first, last)], 1)


def flat(x):
    return x.reshape(x.shape[0] * x.shape[1], x.shape[2])


def step_kernel(old, group, own_ref, other_ref, *refs):
    if old:
        rows_ref, inverse_ref, spread_ref, lane_ref, best_in = refs[:5]
        refs = refs[5:]
    rows_out, inverse_out, spread_out, lane_out, best_out, token_ref, running = refs
    fresh = rows_out.shape[0]
    count = fresh * LANES
    full, rest = old // group, old % group
    step = pl.program_id(0)

    @pl.when(step == 0)
    def _():
        for side, ref in ((0, own_ref), (1, other_ref)):
            keys = new_keys(ref, count)
            for slot in range(fresh):
                cut = slice(slot * LANES, (slot + 1) * LANES)
                rows_out[slot, side] = ref[cut]
                x = ref[cut].astype(jnp.float32)
                inverse = lax.rsqrt(jnp.sum(x * x, 1, keepdims=True) + EPSILON)
                inverse_out[slot, side] = jnp.broadcast_to(inverse, (LANES, LANES))
                spread_out[slot, side] = jnp.transpose(
                    jnp.broadcast_to(keys[:, cut], (LANES, LANES))
                )
                if side == 0:
                    lane_out[slot] = jnp.broadcast_to(keys[:, cut], (8, LANES))
        running[...] = jnp.full(running.shape, MASKED, jnp.float32)

    own_key = new_keys(own_ref, count)

    def against_new(queries, query_key, best):
        for slot in range(fresh):
            best = jnp.maximum(
                best,
                best_of(flat(rows_out[slot]), flat(inverse_out[slot]), flat(spread_out[slot]),
                        queries, query_key),
            )
        return best

    def visit(slots):
        old_key = joined(lane_ref, 0, slots)[0:1]
        old_best = against_new(flat(rows_ref[:slots, 0]), old_key, joined(best_in, 0, slots))
        for slot in range(slots):
            best_out[slot] = old_best[:, slot * LANES : (slot + 1) * LANES]
        best = running[...]
        for slot in range(slots):
            best = jnp.maximum(
                best,
                best_of(flat(rows_ref[slot]), flat(inverse_ref[slot]), flat(spread_ref[slot]),
                        own_ref[:count], own_key),
            )
        running[...] = best

    if full:

        @pl.when(step < full)
        def _():
            visit(group)

    @pl.when(step == full)
    def _():
        if rest:
            visit(rest)
        best = against_new(own_ref[:count], own_key, running[...])
        for slot in range(fresh):
            best_out[rest + slot] = best[:, slot * LANES : (slot + 1) * LANES]
        token_ref[...] = best[:, :LANES]


def match_step(old, group, room, own, other, state):
    count, width = own.shape[0] - 8, own.shape[1]
    fresh = count // LANES
    full, rest = old // group, old % group

    def whole(shape):
        return pl.BlockSpec(shape, lambda i: (0,) * len(shape))

    def old_block(shape):
        last = max(-(-old // group) - 1, 0)
        return pl.BlockSpec(
            (group,) + shape, lambda i: (jnp.minimum(i, last),) + (0,) * len(shape)
        )

    def new_block(shape):
        return pl.BlockSpec((fresh,) + shape, lambda i: (old // fresh,) + (0,) * len(shape))

    shapes = ((2, LANES, width), (2, LANES, LANES), (2, LANES, LANES), (8, LANES), (8, LANES))
    dtypes = (own.dtype, jnp.float32, jnp.int32, jnp.int32, jnp.float32)
    in_specs = [whole(own.shape), whole(own.shape)]
    if old:
        in_specs += [old_block(shape) for shape in shapes]
    pairs = 2 * (2 * old + fresh) * count * LANES
    return pl.pallas_call(
        functools.partial(step_kernel, old, group),
        grid=(full + 1,),
        in_specs=in_specs,
        out_specs=tuple(new_block(shape) for shape in shapes[:4])
        + (pl.BlockSpec((group, 8, LANES), lambda i: (i, 0, 0)), whole((8, LANES))),
        out_shape=tuple(
            jax.ShapeDtypeStruct((room,) + shape, dtype) for shape, dtype in zip(shapes, dtypes)
        )
        + (jax.ShapeDtypeStruct((8, LANES), jnp.float32),),
        scratch_shapes=[pltpu.VMEM((8, count), jnp.float32)],
        input_output_aliases={2 + i: i for i in range(5)} if old else {},
        compiler_params=pltpu.CompilerParams(vmem_limit_bytes=MATCH_LIMIT),
        cost_estimate=pl.CostEstimate(
            flops=2 * pairs * width, bytes_accessed=4 * (old + 1) * LANES * width, transcendentals=0
        ),
        name="match_step",
    )(own, other, *state)


def answer_kernel(chip_ref, block_rows, table_ref, pos_ref, inverse_ref, out_ref):
    rows = pos_ref.shape[1]
    chunk = 512
    table = table_ref[...]
    high = table.astype(jnp.bfloat16)
    rest = table - high.astype(jnp.float32)
    middle = rest.astype(jnp.bfloat16)
    low = (rest - middle.astype(jnp.float32)).astype(jnp.bfloat16)
    high_iota = lax.broadcasted_iota(jnp.int32, (rows // LANES, chunk), 0)
    low_iota = lax.broadcasted_iota(jnp.int32, (LANES, chunk), 0)
    for start in range(0, rows, chunk):
        position = pos_ref[:, start : start + chunk] ^ (chip_ref[0] * block_rows)
        hot = one_hot((position >> 7) == high_iota)
        values = sum(
            lax.dot_general(part, hot, (((0,), (0,)), ((), ())), preferred_element_type=jnp.float32)
            for part in (high, middle, low)
        )
        best = jnp.sum(
            jnp.where((position & 127) == low_iota, values, 0.0), 0, keepdims=True
        )
        out_ref[:, start : start + chunk] = jnp.maximum(
            best * inverse_ref[:, start : start + chunk], -1.0
        )


def answer_rows(chip, table, position, inverse, block_rows):
    rows = position.shape[1]

    def body(chip_ref, *refs):
        answer_kernel(chip_ref, block_rows, *refs)

    return pl.pallas_call(
        body,
        in_specs=[pl.BlockSpec(memory_space=pltpu.SMEM)] + [pl.BlockSpec(memory_space=pltpu.VMEM)] * 3,
        out_shape=jax.ShapeDtypeStruct((1, rows), jnp.float32),
        compiler_params=params(),
        name="answer_rows",
    )(chip, table, position, inverse)


def after_kernel(x_ref, token_ref, out_ref):
    pass


def after(x, token):
    return pl.pallas_call(
        after_kernel,
        in_specs=[pl.BlockSpec(memory_space=pl.ANY)] * 2,
        out_specs=pl.BlockSpec(memory_space=pl.ANY),
        out_shape=jax.ShapeDtypeStruct(x.shape, x.dtype),
        input_output_aliases={0: 0},
        compiler_params=pltpu.CompilerParams(vmem_limit_bytes=1024 * 1024),
        cost_estimate=pl.CostEstimate(flops=0, bytes_accessed=0, transcendentals=0),
        name="after",
    )(x, token)


def on_device(embeddings, cluster_ids, member_ranks):
    rows, width = embeddings.shape
    owners = lax.axis_size("owner")
    chips = owners // 2
    block = rows // chips
    group = block // LANES
    room = rows // LANES
    chip = (lax.axis_index("owner") // 2).astype(jnp.int32)

    def across(x, d):
        return lax.ppermute(x, "owner", [(i, i ^ (2 * d)) for i in range(owners)])

    def swap(x):
        return lax.ppermute(x, "owner", [(i, i ^ 1) for i in range(owners)])

    near = list(range(1, chips // 2))
    far = list(range(chips // 2, chips))
    order = far[:2]
    for a, b in zip(near, far[2:-1]):
        order += [a, b]
    order += near[len(far[2:-1]) :]
    pieces = [(d, 0, block) for d in order]
    cuts = [block // 2] + ([block // 4] * 2 if block >= 4 * LANES else [block // 2])
    at = 0
    for size in cuts:
        pieces.append((far[-1], at, size))
        at += size
    rest = [(0, 0, block)] + pieces[1:]

    def begin(d, at):
        return (chip ^ d) * block + at

    position, keys = order_rows(cluster_ids, member_ranks, chips * GROUP)
    first = pick_first(begin(order[0], 0).reshape(1), keys, position, embeddings, block)
    own = {pieces[0]: across(first, order[0])}
    starts = jnp.stack([begin(d, at) for d, at, size in rest])
    *picked, inverse = pick_rest(starts, keys, position, embeddings, [size for d, at, size in rest])
    sent = dict(zip(rest, picked))
    visits = [rest[0]] + pieces
    own[visits[0]] = picked[0]
    other = {visits[0]: swap(picked[0])}
    tokens = {}
    state = ()
    old = 0
    spots = {}
    for turn, piece in enumerate(visits):
        if turn == 0:
            for ahead in visits[2:5]:
                own[ahead] = across(sent[ahead], ahead[0])
            other[visits[1]] = swap(own[visits[1]])
        else:
            if turn + 4 <= len(visits):
                for ahead in visits[turn + 4 : turn + 5]:
                    own[ahead] = across(after(sent[ahead], tokens[turn - 1]), ahead[0])
            if turn + 1 < len(visits):
                ahead = visits[turn + 1]
                own[ahead] = after(own[ahead], tokens[turn - 1])
                other[ahead] = swap(own[ahead])
        spots[piece] = old
        *state, tokens[turn] = match_step(old, group, room, own[piece], other[piece], state)
        old += piece[2] // LANES
    best = jnp.max(state[4], 1)
    table = jnp.concatenate(
        [
            best[spots[piece] : spots[piece] + piece[2] // LANES]
            for piece in sorted([rest[0]] + pieces)
        ],
        0,
    ).reshape(chips, group, LANES)
    bit = 1
    while bit < chips:
        split = table.reshape(chips // (2 * bit), 2, bit, group, LANES)
        got = across(split[:, 1], bit)
        table = jnp.stack([split[:, 0], got], 1).reshape(chips, group, LANES)
        bit *= 2
    table = table.reshape(rows // LANES, LANES)
    answer = answer_rows(chip.reshape(1), table, position, inverse, block)
    return answer.reshape(rows)


def solution(mesh):
    in_specs = (P(("parts", "owner"), None), P(("parts", "owner")), P(("parts", "owner")))
    out_specs = P(("parts", "owner"))
    return jax.shard_map(
        on_device, mesh=mesh, in_specs=in_specs, out_specs=out_specs, check_vma=False
    )
```

```python
import functools

import jax
import jax.numpy as jnp
from jax import lax
from jax.experimental import pallas as pl
from jax.experimental.pallas import tpu as pltpu
from jax.sharding import PartitionSpec as P

CL_DEV = 4
CMAX = 2048
EPSILON = 1e-06
MASKED = -30000.0
GROUP = 2 * CL_DEV
LANES = 128
VMEM_LIMIT = 24 * 1024 * 1024
MATCH_LIMIT = 20 * 1024 * 1024


def params():
    return pltpu.CompilerParams(vmem_limit_bytes=VMEM_LIMIT)


def nt_dot(a, b):
    return lax.dot_general(a, b, (((1,), (1,)), ((), ())), preferred_element_type=jnp.float32)


def one_hot(condition):
    return jnp.where(condition, 1.0, 0.0).astype(jnp.bfloat16)


def tile_lanes(x, times):
    return jnp.concatenate([x] * times, 1)


def order_kernel(ids_ref, ranks_ref, pos_ref, keys_ref, local_ref):
    rows = ids_ref.shape[1]
    clusters = local_ref.shape[0]
    chunk = 256
    cluster_iota = lax.broadcasted_iota(jnp.int32, (clusters, chunk), 0)
    before = one_hot(
        lax.broadcasted_iota(jnp.int32, (chunk, chunk), 0)
        < lax.broadcasted_iota(jnp.int32, (chunk, chunk), 1)
    )
    ones = jnp.ones((chunk, LANES), jnp.bfloat16)
    count = jnp.zeros((clusters, LANES), jnp.float32)
    for start in range(0, rows, chunk):
        hot = one_hot(ids_ref[:, start : start + chunk] == cluster_iota)
        prefix = jnp.dot(hot, before, preferred_element_type=jnp.float32)
        local_ref[:, start : start + chunk] = prefix + tile_lanes(count, chunk // LANES)
        count += jnp.dot(hot, ones, preferred_element_type=jnp.float32)
    lower = one_hot(
        lax.broadcasted_iota(jnp.int32, (clusters, clusters), 1)
        < lax.broadcasted_iota(jnp.int32, (clusters, clusters), 0)
    )
    offset = jnp.dot(lower, count.astype(jnp.bfloat16), preferred_element_type=jnp.float32)
    offset = tile_lanes(offset, chunk // LANES)
    high_rows = rows // LANES
    table = jnp.zeros((2 * high_rows, LANES), jnp.float32)
    high_iota = lax.broadcasted_iota(jnp.int32, (high_rows, chunk), 0)
    low_iota = lax.broadcasted_iota(jnp.int32, (LANES, chunk), 0)
    for start in range(0, rows, chunk):
        ids = ids_ref[:, start : start + chunk]
        place = jnp.where(
            ids == cluster_iota, local_ref[:, start : start + chunk] + offset, 0.0
        )
        position = jnp.sum(place, 0, keepdims=True).astype(jnp.int32)
        pos_ref[:, start : start + chunk] = position
        key = (ids & (GROUP - 1)) * CMAX + ranks_ref[:, start : start + chunk]
        high_hot = (position >> 7) == high_iota
        key_high = (key >> 7).astype(jnp.float32)
        key_low = (key & 127).astype(jnp.float32)
        left = jnp.concatenate(
            [jnp.where(high_hot, key_high, 0.0), jnp.where(high_hot, key_low, 0.0)], 0
        ).astype(jnp.bfloat16)
        table += nt_dot(left, one_hot((position & 127) == low_iota))
    keys = (table[:high_rows] * 128.0 + table[high_rows:]).astype(jnp.int32)
    for row in range(high_rows):
        keys_ref[row] = jnp.broadcast_to(keys[row : row + 1], (8, LANES))


def order_rows(ids, ranks, clusters):
    rows = ids.shape[0]
    return pl.pallas_call(
        order_kernel,
        out_shape=(
            jax.ShapeDtypeStruct((1, rows), jnp.int32),
            jax.ShapeDtypeStruct((rows // LANES, 8, LANES), jnp.int32),
        ),
        scratch_shapes=[pltpu.VMEM((clusters, rows), jnp.float32)],
        compiler_params=params(),
        cost_estimate=pl.CostEstimate(flops=10**10, bytes_accessed=10**6, transcendentals=0),
        name="order_rows",
    )(ids.reshape(1, rows), ranks.reshape(1, rows))


def key_rows(keys_ref, row, count, width):
    upper = lax.broadcasted_iota(jnp.int32, (8, LANES), 0) == 0
    tiles = []
    for i in range(count):
        key = keys_ref[row + i]
        tiles.append(jnp.where(upper, key >> 7, key & 127).astype(jnp.float32))
    tiles += [jnp.zeros((8, LANES), jnp.float32)] * (width // LANES - count)
    return jnp.concatenate(tiles, 1).astype(jnp.bfloat16)


def inverse_lanes(x):
    x = x.astype(jnp.float32)
    inverse = lax.rsqrt(jnp.sum(x * x, 1, keepdims=True) + EPSILON)
    return jnp.transpose(jnp.broadcast_to(inverse, (LANES, LANES)))[0:1]


def pick_kernel(counts, norms, start_ref, keys_ref, pos_ref, rows_ref, before_ref, *refs):
    outs = refs[: len(counts)]
    rows, width = rows_ref.shape
    for k, count in enumerate(counts):
        out_ref = outs[k]
        start = start_ref[k]
        tile = min(count, 256)

        def one_tile(i, carry, out_ref=out_ref, start=start, tile=tile):
            target = lax.broadcasted_iota(jnp.int32, (tile, rows), 0) + (start + i * tile)
            picked = jnp.dot(
                one_hot(pos_ref[...] == target), rows_ref[...], preferred_element_type=jnp.float32
            )
            out_ref[pl.ds(pl.multiple_of(i * tile, tile), tile)] = picked.astype(out_ref.dtype)
            return carry

        lax.fori_loop(0, count // tile, one_tile, 0)
        out_ref[count:] = key_rows(keys_ref, start // LANES, count // LANES, width)

    if norms:
        for at in range(0, rows, LANES):
            refs[-1][:, at : at + LANES] = inverse_lanes(rows_ref[at : at + LANES])


def pick_blocks(starts, keys, position, embeddings, before, counts, norms):
    rows, width = embeddings.shape
    vmem = pl.BlockSpec(memory_space=pltpu.VMEM)
    return pl.pallas_call(
        functools.partial(pick_kernel, counts, norms),
        in_specs=[pl.BlockSpec(memory_space=pltpu.SMEM), vmem, vmem, vmem]
        + [pl.BlockSpec(memory_space=pl.ANY)],
        out_shape=tuple(jax.ShapeDtypeStruct((count + 8, width), embeddings.dtype) for count in counts)
        + (jax.ShapeDtypeStruct((1, rows), jnp.float32),) * norms,
        out_specs=(vmem,) * (len(counts) + norms),
        compiler_params=params(),
        cost_estimate=pl.CostEstimate(
            flops=2 * sum(counts) * rows * width, bytes_accessed=4 * rows * width, transcendentals=0
        ),
        name="pick_blocks",
    )(starts, keys, position, embeddings, before)


def new_keys(ref, count):
    parts = ref[count : count + 8, :count].astype(jnp.float32)
    return (parts[0:1] * 128.0 + parts[1:2]).astype(jnp.int32)


def best_of(columns, column_inverse, column_key, queries, query_key):
    count = queries.shape[0]
    scores = nt_dot(columns, queries)
    scores = scores * tile_lanes(column_inverse, count // LANES)
    rank = query_key & (CMAX - 1)
    base = query_key - rank
    earlier = (tile_lanes(column_key, count // LANES) ^ base) < rank
    scores = jnp.where(earlier, scores, MASKED)
    return jnp.max(scores.reshape(scores.shape[0] // 8, 8, count), 0)


def joined(ref, first, last):
    return jnp.concatenate([ref[i] for i in range(first, last)], 1)


def flat(x):
    return x.reshape(x.shape[0] * x.shape[1], x.shape[2])


def step_kernel(old, group, own_ref, other_ref, *refs):
    if old:
        rows_ref, inverse_ref, spread_ref, lane_ref, best_in = refs[:5]
        refs = refs[5:]
    rows_out, inverse_out, spread_out, lane_out, best_out, token_ref, running = refs
    fresh = rows_out.shape[0]
    count = fresh * LANES
    full, rest = old // group, old % group
    step = pl.program_id(0)

    @pl.when(step == 0)
    def _():
        for side, ref in ((0, own_ref), (1, other_ref)):
            keys = new_keys(ref, count)
            for slot in range(fresh):
                cut = slice(slot * LANES, (slot + 1) * LANES)
                rows_out[slot, side] = ref[cut]
                x = ref[cut].astype(jnp.float32)
                inverse = lax.rsqrt(jnp.sum(x * x, 1, keepdims=True) + EPSILON)
                inverse_out[slot, side] = jnp.broadcast_to(inverse, (LANES, LANES))
                spread_out[slot, side] = jnp.transpose(
                    jnp.broadcast_to(keys[:, cut], (LANES, LANES))
                )
                if side == 0:
                    lane_out[slot] = jnp.broadcast_to(keys[:, cut], (8, LANES))
        running[...] = jnp.full(running.shape, MASKED, jnp.float32)

    own_key = new_keys(own_ref, count)

    def against_new(queries, query_key, best):
        for slot in range(fresh):
            best = jnp.maximum(
                best,
                best_of(flat(rows_out[slot]), flat(inverse_out[slot]), flat(spread_out[slot]),
                        queries, query_key),
            )
        return best

    def visit(slots):
        old_key = joined(lane_ref, 0, slots)[0:1]
        old_best = against_new(flat(rows_ref[:slots, 0]), old_key, joined(best_in, 0, slots))
        for slot in range(slots):
            best_out[slot] = old_best[:, slot * LANES : (slot + 1) * LANES]
        best = running[...]
        for slot in range(slots):
            best = jnp.maximum(
                best,
                best_of(flat(rows_ref[slot]), flat(inverse_ref[slot]), flat(spread_ref[slot]),
                        own_ref[:count], own_key),
            )
        running[...] = best

    if full:

        @pl.when(step < full)
        def _():
            visit(group)

    @pl.when(step == full)
    def _():
        if rest:
            visit(rest)
        best = against_new(own_ref[:count], own_key, running[...])
        for slot in range(fresh):
            best_out[rest + slot] = best[:, slot * LANES : (slot + 1) * LANES]
        token_ref[...] = best[:, :LANES]


def match_step(old, group, room, own, other, state):
    count, width = own.shape[0] - 8, own.shape[1]
    fresh = count // LANES
    full, rest = old // group, old % group

    def whole(shape):
        return pl.BlockSpec(shape, lambda i: (0,) * len(shape))

    def old_block(shape):
        last = max(-(-old // group) - 1, 0)
        return pl.BlockSpec(
            (group,) + shape, lambda i: (jnp.minimum(i, last),) + (0,) * len(shape)
        )

    def new_block(shape):
        return pl.BlockSpec((fresh,) + shape, lambda i: (old // fresh,) + (0,) * len(shape))

    shapes = ((2, LANES, width), (2, LANES, LANES), (2, LANES, LANES), (8, LANES), (8, LANES))
    dtypes = (own.dtype, jnp.float32, jnp.int32, jnp.int32, jnp.float32)
    in_specs = [whole(own.shape), whole(own.shape)]
    if old:
        in_specs += [old_block(shape) for shape in shapes]
    return pl.pallas_call(
        functools.partial(step_kernel, old, group),
        grid=(full + 1,),
        in_specs=in_specs,
        out_specs=tuple(new_block(shape) for shape in shapes[:4])
        + (pl.BlockSpec((group, 8, LANES), lambda i: (i, 0, 0)), whole((8, LANES))),
        out_shape=tuple(
            jax.ShapeDtypeStruct((room,) + shape, dtype) for shape, dtype in zip(shapes, dtypes)
        )
        + (jax.ShapeDtypeStruct((8, LANES), jnp.float32),),
        scratch_shapes=[pltpu.VMEM((8, count), jnp.float32)],
        input_output_aliases={2 + i: i for i in range(5)} if old else {},
        compiler_params=pltpu.CompilerParams(vmem_limit_bytes=MATCH_LIMIT),
        cost_estimate=pl.CostEstimate(
            flops=3 * 10**9 if old >= 3 * group else LANES, bytes_accessed=LANES, transcendentals=0
        ),
        name="match_step",
    )(own, other, *state)


def answer_kernel(chip_ref, block_rows, table_ref, pos_ref, inverse_ref, out_ref):
    rows = pos_ref.shape[1]
    chunk = 512
    table = table_ref[...]
    high = table.astype(jnp.bfloat16)
    rest = table - high.astype(jnp.float32)
    middle = rest.astype(jnp.bfloat16)
    low = (rest - middle.astype(jnp.float32)).astype(jnp.bfloat16)
    high_iota = lax.broadcasted_iota(jnp.int32, (rows // LANES, chunk), 0)
    low_iota = lax.broadcasted_iota(jnp.int32, (LANES, chunk), 0)
    for start in range(0, rows, chunk):
        position = pos_ref[:, start : start + chunk] ^ (chip_ref[0] * block_rows)
        hot = one_hot((position >> 7) == high_iota)
        values = sum(
            lax.dot_general(part, hot, (((0,), (0,)), ((), ())), preferred_element_type=jnp.float32)
            for part in (high, middle, low)
        )
        best = jnp.sum(
            jnp.where((position & 127) == low_iota, values, 0.0), 0, keepdims=True
        )
        out_ref[:, start : start + chunk] = jnp.maximum(
            best * inverse_ref[:, start : start + chunk], -1.0
        )


def answer_rows(chip, table, position, inverse, block_rows):
    rows = position.shape[1]

    def body(chip_ref, *refs):
        answer_kernel(chip_ref, block_rows, *refs)

    return pl.pallas_call(
        body,
        in_specs=[pl.BlockSpec(memory_space=pltpu.SMEM)] + [pl.BlockSpec(memory_space=pltpu.VMEM)] * 3,
        out_shape=jax.ShapeDtypeStruct((1, rows), jnp.float32),
        compiler_params=params(),
        name="answer_rows",
    )(chip, table, position, inverse)


def after_kernel(x_ref, token_ref, out_ref):
    pass


def after(x, token):
    return pl.pallas_call(
        after_kernel,
        in_specs=[pl.BlockSpec(memory_space=pl.ANY)] * 2,
        out_specs=pl.BlockSpec(memory_space=pl.ANY),
        out_shape=jax.ShapeDtypeStruct(x.shape, x.dtype),
        input_output_aliases={0: 0},
        compiler_params=pltpu.CompilerParams(vmem_limit_bytes=1024 * 1024),
        cost_estimate=pl.CostEstimate(flops=0, bytes_accessed=0, transcendentals=0),
        name="after",
    )(x, token)


def on_device(embeddings, cluster_ids, member_ranks):
    rows, width = embeddings.shape
    owners = lax.axis_size("owner")
    chips = owners // 2
    block = rows // chips
    group = block // LANES
    room = rows // LANES
    chip = (lax.axis_index("owner") // 2).astype(jnp.int32)

    def across(x, d):
        return lax.ppermute(x, "owner", [(i, i ^ (2 * d)) for i in range(owners)])

    def swap(x):
        return lax.ppermute(x, "owner", [(i, i ^ 1) for i in range(owners)])

    local = (0, 0, block)
    near = [(d, 0, block) for d in range(1, chips // 2)]
    far = [(d, 0, block) for d in range(chips // 2, chips - 1)]
    last = [(chips - 1, 0, block)]
    rounds = [[local]] + [list(pair) for pair in zip(near, far)] + [[piece] for piece in last]
    visits = [piece for pieces in rounds for piece in pieces]
    follow = {rounds[turn][-1]: rounds[turn + 2] for turn in range(1, len(rounds) - 2)}
    batches = [rounds[1][::-1], [local, *visits[3:]]]

    position, keys = order_rows(cluster_ids, member_ranks, chips * GROUP)
    sent = {}
    for turn, batch in enumerate(batches):
        starts = jnp.stack([(chip ^ d) * block + at for d, at, size in batch])
        counts = [size for d, at, size in batch]
        before = picked[0] if turn else keys
        picked = pick_blocks(
            starts, keys, position, embeddings, before, counts, turn + 1 == len(batches)
        )
        sent.update(zip(batch, picked))
    inverse = picked[-1]
    own = {piece: across(sent[piece], piece[0]) for piece in visits[1:5]}
    own[local] = sent[local]
    state = ()
    old = 0
    spots = {}
    token = None
    for turn, pieces in enumerate(rounds):
        if turn > 1:
            for piece in pieces:
                own[piece] = after(own[piece], token)
        other = [swap(own[piece]) for piece in pieces]
        for piece, twin in zip(pieces, other):
            spots[piece] = old
            *state, token = match_step(old, group, room, own[piece], twin, state)
            old += piece[2] // LANES
            for ahead in follow.get(piece, ()):
                own[ahead] = across(after(sent[ahead], token), ahead[0])
    best = jnp.max(state[4], 1)
    table = jnp.concatenate(
        [
            best[spots[piece] : spots[piece] + piece[2] // LANES]
            for piece in sorted(visits)
        ],
        0,
    ).reshape(chips, group, LANES)
    bit = 1
    while bit < chips:
        split = table.reshape(chips // (2 * bit), 2, bit, group, LANES)
        got = across(split[:, 1], bit)
        table = jnp.stack([split[:, 0], got], 1).reshape(chips, group, LANES)
        bit *= 2
    table = table.reshape(rows // LANES, LANES)
    answer = answer_rows(chip.reshape(1), table, position, inverse, block)
    return answer.reshape(rows)


def solution(mesh):
    in_specs = (P(("parts", "owner"), None), P(("parts", "owner")), P(("parts", "owner")))
    out_specs = P(("parts", "owner"))
    return jax.shard_map(
        on_device, mesh=mesh, in_specs=in_specs, out_specs=out_specs, check_vma=False
    )
```

```python
import functools

import jax
import jax.numpy as jnp
from jax import lax
from jax.experimental import pallas as pl
from jax.experimental.pallas import tpu as pltpu
from jax.sharding import PartitionSpec as P

CL_DEV = 4
CMAX = 2048
EPSILON = 1e-06
MASKED = -30000.0
GROUP = 2 * CL_DEV
LANES = 128
VMEM_LIMIT = 24 * 1024 * 1024
MATCH_LIMIT = 20 * 1024 * 1024


def params():
    return pltpu.CompilerParams(vmem_limit_bytes=VMEM_LIMIT)


def nt_dot(a, b):
    return lax.dot_general(a, b, (((1,), (1,)), ((), ())), preferred_element_type=jnp.float32)


def one_hot(condition):
    return jnp.where(condition, 1.0, 0.0).astype(jnp.bfloat16)


def tile_lanes(x, times):
    return jnp.concatenate([x] * times, 1)


def order_kernel(ids_ref, ranks_ref, pos_ref, keys_ref, local_ref):
    rows = ids_ref.shape[1]
    clusters = local_ref.shape[0]
    chunk = 256
    cluster_iota = lax.broadcasted_iota(jnp.int32, (clusters, chunk), 0)
    before = one_hot(
        lax.broadcasted_iota(jnp.int32, (chunk, chunk), 0)
        < lax.broadcasted_iota(jnp.int32, (chunk, chunk), 1)
    )
    ones = jnp.ones((chunk, LANES), jnp.bfloat16)
    count = jnp.zeros((clusters, LANES), jnp.float32)
    for start in range(0, rows, chunk):
        hot = one_hot(ids_ref[:, start : start + chunk] == cluster_iota)
        prefix = jnp.dot(hot, before, preferred_element_type=jnp.float32)
        local_ref[:, start : start + chunk] = prefix + tile_lanes(count, chunk // LANES)
        count += jnp.dot(hot, ones, preferred_element_type=jnp.float32)
    lower = one_hot(
        lax.broadcasted_iota(jnp.int32, (clusters, clusters), 1)
        < lax.broadcasted_iota(jnp.int32, (clusters, clusters), 0)
    )
    offset = jnp.dot(lower, count.astype(jnp.bfloat16), preferred_element_type=jnp.float32)
    offset = tile_lanes(offset, chunk // LANES)
    high_rows = rows // LANES
    table = jnp.zeros((2 * high_rows, LANES), jnp.float32)
    high_iota = lax.broadcasted_iota(jnp.int32, (high_rows, chunk), 0)
    low_iota = lax.broadcasted_iota(jnp.int32, (LANES, chunk), 0)
    for start in range(0, rows, chunk):
        ids = ids_ref[:, start : start + chunk]
        place = jnp.where(
            ids == cluster_iota, local_ref[:, start : start + chunk] + offset, 0.0
        )
        position = jnp.sum(place, 0, keepdims=True).astype(jnp.int32)
        pos_ref[:, start : start + chunk] = position
        key = (ids & (GROUP - 1)) * CMAX + ranks_ref[:, start : start + chunk]
        high_hot = (position >> 7) == high_iota
        key_high = (key >> 7).astype(jnp.float32)
        key_low = (key & 127).astype(jnp.float32)
        left = jnp.concatenate(
            [jnp.where(high_hot, key_high, 0.0), jnp.where(high_hot, key_low, 0.0)], 0
        ).astype(jnp.bfloat16)
        table += nt_dot(left, one_hot((position & 127) == low_iota))
    keys = (table[:high_rows] * 128.0 + table[high_rows:]).astype(jnp.int32)
    for row in range(high_rows):
        keys_ref[row] = jnp.broadcast_to(keys[row : row + 1], (8, LANES))


def order_rows(ids, ranks, clusters):
    rows = ids.shape[0]
    return pl.pallas_call(
        order_kernel,
        out_shape=(
            jax.ShapeDtypeStruct((1, rows), jnp.int32),
            jax.ShapeDtypeStruct((rows // LANES, 8, LANES), jnp.int32),
        ),
        scratch_shapes=[pltpu.VMEM((clusters, rows), jnp.float32)],
        compiler_params=params(),
        cost_estimate=pl.CostEstimate(flops=10**10, bytes_accessed=10**6, transcendentals=0),
        name="order_rows",
    )(ids.reshape(1, rows), ranks.reshape(1, rows))


def key_rows(keys_ref, row, count, width):
    upper = lax.broadcasted_iota(jnp.int32, (8, LANES), 0) == 0
    tiles = []
    for i in range(count):
        key = keys_ref[row + i]
        tiles.append(jnp.where(upper, key >> 7, key & 127).astype(jnp.float32))
    tiles += [jnp.zeros((8, LANES), jnp.float32)] * (width // LANES - count)
    return jnp.concatenate(tiles, 1).astype(jnp.bfloat16)


def inverse_lanes(x):
    x = x.astype(jnp.float32)
    inverse = lax.rsqrt(jnp.sum(x * x, 1, keepdims=True) + EPSILON)
    return jnp.transpose(jnp.broadcast_to(inverse, (LANES, LANES)))[0:1]


def pick_kernel(counts, norms, start_ref, keys_ref, pos_ref, rows_ref, before_ref, *refs):
    outs = refs[: len(counts)]
    rows, width = rows_ref.shape
    for k, count in enumerate(counts):
        out_ref = outs[k]
        start = start_ref[k]
        tile = min(count, 256)

        def one_tile(i, carry, out_ref=out_ref, start=start, tile=tile):
            target = lax.broadcasted_iota(jnp.int32, (tile, rows), 0) + (start + i * tile)
            picked = jnp.dot(
                one_hot(pos_ref[...] == target), rows_ref[...], preferred_element_type=jnp.float32
            )
            out_ref[pl.ds(pl.multiple_of(i * tile, tile), tile)] = picked.astype(out_ref.dtype)
            return carry

        lax.fori_loop(0, count // tile, one_tile, 0)
        out_ref[count:] = key_rows(keys_ref, start // LANES, count // LANES, width)

    if norms:
        for at in range(0, rows, LANES):
            refs[-1][:, at : at + LANES] = inverse_lanes(rows_ref[at : at + LANES])


def pick_blocks(starts, keys, position, embeddings, before, counts, norms):
    rows, width = embeddings.shape
    vmem = pl.BlockSpec(memory_space=pltpu.VMEM)
    return pl.pallas_call(
        functools.partial(pick_kernel, counts, norms),
        in_specs=[pl.BlockSpec(memory_space=pltpu.SMEM), vmem, vmem, vmem]
        + [pl.BlockSpec(memory_space=pl.ANY)],
        out_shape=tuple(jax.ShapeDtypeStruct((count + 8, width), embeddings.dtype) for count in counts)
        + (jax.ShapeDtypeStruct((1, rows), jnp.float32),) * norms,
        out_specs=(vmem,) * (len(counts) + norms),
        compiler_params=params(),
        cost_estimate=pl.CostEstimate(
            flops=2 * sum(counts) * rows * width, bytes_accessed=4 * rows * width, transcendentals=0
        ),
        name="pick_blocks",
    )(starts, keys, position, embeddings, before)


def new_keys(ref, count):
    parts = ref[count : count + 8, :count].astype(jnp.float32)
    return (parts[0:1] * 128.0 + parts[1:2]).astype(jnp.int32)


def best_of(columns, column_inverse, column_key, queries, query_key):
    count = queries.shape[0]
    scores = nt_dot(columns, queries)
    scores = scores * tile_lanes(column_inverse, count // LANES)
    rank = query_key & (CMAX - 1)
    base = query_key - rank
    earlier = (tile_lanes(column_key, count // LANES) ^ base) < rank
    scores = jnp.where(earlier, scores, MASKED)
    return jnp.max(scores.reshape(scores.shape[0] // 8, 8, count), 0)


def joined(ref, first, last):
    return jnp.concatenate([ref[i] for i in range(first, last)], 1)


def flat(x):
    return x.reshape(x.shape[0] * x.shape[1], x.shape[2])


def step_kernel(old, group, own_ref, other_ref, *refs):
    if old:
        rows_ref, inverse_ref, spread_ref, lane_ref, best_in = refs[:5]
        refs = refs[5:]
    rows_out, inverse_out, spread_out, lane_out, best_out, token_ref, running = refs
    fresh = rows_out.shape[0]
    count = fresh * LANES
    full, rest = old // group, old % group
    step = pl.program_id(0)

    @pl.when(step == 0)
    def _():
        for side, ref in ((0, own_ref), (1, other_ref)):
            keys = new_keys(ref, count)
            for slot in range(fresh):
                cut = slice(slot * LANES, (slot + 1) * LANES)
                rows_out[slot, side] = ref[cut]
                x = ref[cut].astype(jnp.float32)
                inverse = lax.rsqrt(jnp.sum(x * x, 1, keepdims=True) + EPSILON)
                inverse_out[slot, side] = jnp.broadcast_to(inverse, (LANES, LANES))
                spread_out[slot, side] = jnp.transpose(
                    jnp.broadcast_to(keys[:, cut], (LANES, LANES))
                )
                if side == 0:
                    lane_out[slot] = jnp.broadcast_to(keys[:, cut], (8, LANES))
        running[...] = jnp.full(running.shape, MASKED, jnp.float32)

    own_key = new_keys(own_ref, count)

    def against_new(queries, query_key, best):
        for slot in range(fresh):
            best = jnp.maximum(
                best,
                best_of(flat(rows_out[slot]), flat(inverse_out[slot]), flat(spread_out[slot]),
                        queries, query_key),
            )
        return best

    def visit(slots):
        old_key = joined(lane_ref, 0, slots)[0:1]
        old_best = against_new(flat(rows_ref[:slots, 0]), old_key, joined(best_in, 0, slots))
        for slot in range(slots):
            best_out[slot] = old_best[:, slot * LANES : (slot + 1) * LANES]
        best = running[...]
        for slot in range(slots):
            best = jnp.maximum(
                best,
                best_of(flat(rows_ref[slot]), flat(inverse_ref[slot]), flat(spread_ref[slot]),
                        own_ref[:count], own_key),
            )
        running[...] = best

    if full:

        @pl.when(step < full)
        def _():
            visit(group)

    @pl.when(step == full)
    def _():
        if rest:
            visit(rest)
        best = against_new(own_ref[:count], own_key, running[...])
        for slot in range(fresh):
            best_out[rest + slot] = best[:, slot * LANES : (slot + 1) * LANES]
        token_ref[...] = best[:, :LANES]


def match_step(old, group, room, own, other, state):
    count, width = own.shape[0] - 8, own.shape[1]
    fresh = count // LANES
    full, rest = old // group, old % group

    def whole(shape):
        return pl.BlockSpec(shape, lambda i: (0,) * len(shape))

    def old_block(shape):
        last = max(-(-old // group) - 1, 0)
        return pl.BlockSpec(
            (group,) + shape, lambda i: (jnp.minimum(i, last),) + (0,) * len(shape)
        )

    def new_block(shape):
        return pl.BlockSpec((fresh,) + shape, lambda i: (old // fresh,) + (0,) * len(shape))

    shapes = ((2, LANES, width), (2, LANES, LANES), (2, LANES, LANES), (8, LANES), (8, LANES))
    dtypes = (own.dtype, jnp.float32, jnp.int32, jnp.int32, jnp.float32)
    in_specs = [whole(own.shape), whole(own.shape)]
    if old:
        in_specs += [old_block(shape) for shape in shapes]
    return pl.pallas_call(
        functools.partial(step_kernel, old, group),
        grid=(full + 1,),
        in_specs=in_specs,
        out_specs=tuple(new_block(shape) for shape in shapes[:4])
        + (pl.BlockSpec((group, 8, LANES), lambda i: (i, 0, 0)), whole((8, LANES))),
        out_shape=tuple(
            jax.ShapeDtypeStruct((room,) + shape, dtype) for shape, dtype in zip(shapes, dtypes)
        )
        + (jax.ShapeDtypeStruct((8, LANES), jnp.float32),),
        scratch_shapes=[pltpu.VMEM((8, count), jnp.float32)],
        input_output_aliases={2 + i: i for i in range(5)} if old else {},
        compiler_params=pltpu.CompilerParams(vmem_limit_bytes=MATCH_LIMIT),
        cost_estimate=pl.CostEstimate(
            flops=3 * 10**9 if old >= 2 * group else LANES, bytes_accessed=LANES, transcendentals=0
        ),
        name="match_step",
    )(own, other, *state)


def answer_kernel(chip_ref, block_rows, table_ref, pos_ref, inverse_ref, out_ref):
    rows = pos_ref.shape[1]
    chunk = 512
    table = table_ref[...]
    high = table.astype(jnp.bfloat16)
    rest = table - high.astype(jnp.float32)
    middle = rest.astype(jnp.bfloat16)
    low = (rest - middle.astype(jnp.float32)).astype(jnp.bfloat16)
    high_iota = lax.broadcasted_iota(jnp.int32, (rows // LANES, chunk), 0)
    low_iota = lax.broadcasted_iota(jnp.int32, (LANES, chunk), 0)
    for start in range(0, rows, chunk):
        position = pos_ref[:, start : start + chunk] ^ (chip_ref[0] * block_rows)
        hot = one_hot((position >> 7) == high_iota)
        values = sum(
            lax.dot_general(part, hot, (((0,), (0,)), ((), ())), preferred_element_type=jnp.float32)
            for part in (high, middle, low)
        )
        best = jnp.sum(
            jnp.where((position & 127) == low_iota, values, 0.0), 0, keepdims=True
        )
        out_ref[:, start : start + chunk] = jnp.maximum(
            best * inverse_ref[:, start : start + chunk], -1.0
        )


def answer_rows(chip, table, position, inverse, block_rows):
    rows = position.shape[1]

    def body(chip_ref, *refs):
        answer_kernel(chip_ref, block_rows, *refs)

    return pl.pallas_call(
        body,
        in_specs=[pl.BlockSpec(memory_space=pltpu.SMEM)] + [pl.BlockSpec(memory_space=pltpu.VMEM)] * 3,
        out_shape=jax.ShapeDtypeStruct((1, rows), jnp.float32),
        compiler_params=params(),
        name="answer_rows",
    )(chip, table, position, inverse)


def after_kernel(x_ref, token_ref, out_ref):
    pass


def after(x, token):
    return pl.pallas_call(
        after_kernel,
        in_specs=[pl.BlockSpec(memory_space=pl.ANY)] * 2,
        out_specs=pl.BlockSpec(memory_space=pl.ANY),
        out_shape=jax.ShapeDtypeStruct(x.shape, x.dtype),
        input_output_aliases={0: 0},
        compiler_params=pltpu.CompilerParams(vmem_limit_bytes=1024 * 1024),
        cost_estimate=pl.CostEstimate(flops=0, bytes_accessed=0, transcendentals=0),
        name="after",
    )(x, token)


def on_device(embeddings, cluster_ids, member_ranks):
    rows, width = embeddings.shape
    owners = lax.axis_size("owner")
    chips = owners // 2
    block = rows // chips
    group = block // LANES
    room = rows // LANES
    chip = (lax.axis_index("owner") // 2).astype(jnp.int32)

    def across(x, d):
        return lax.ppermute(x, "owner", [(i, i ^ (2 * d)) for i in range(owners)])

    def swap(x):
        return lax.ppermute(x, "owner", [(i, i ^ 1) for i in range(owners)])

    local = (0, 0, block)
    near = [(d, 0, block) for d in range(1, chips // 2)]
    far = [(d, 0, block) for d in range(chips // 2, chips - 1)]
    last = (chips - 1, 0, block)
    rounds = [[local], far[:1], [far[1], *near[:2]]]
    rounds += [list(pair) for pair in zip(near[2:], far[2:])] + [[last]]
    visits = [piece for pieces in rounds for piece in pieces]
    follow = {rounds[turn][-1]: rounds[turn + 2] for turn in range(1, len(rounds) - 2)}
    batches = [rounds[1], [local, *visits[2:]]]

    position, keys = order_rows(cluster_ids, member_ranks, chips * GROUP)
    sent = {}
    for turn, batch in enumerate(batches):
        starts = jnp.stack([(chip ^ d) * block + at for d, at, size in batch])
        counts = [size for d, at, size in batch]
        before = picked[0] if turn else keys
        picked = pick_blocks(
            starts, keys, position, embeddings, before, counts, turn + 1 == len(batches)
        )
        sent.update(zip(batch, picked))
    inverse = picked[-1]
    own = {piece: across(sent[piece], piece[0]) for piece in visits[1:5]}
    own[local] = sent[local]
    state = ()
    old = 0
    spots = {}
    token = None
    for turn, pieces in enumerate(rounds):
        if turn > 1:
            for piece in pieces:
                own[piece] = after(own[piece], token)
        other = [swap(own[piece]) for piece in pieces]
        for piece, twin in zip(pieces, other):
            spots[piece] = old
            *state, token = match_step(old, group, room, own[piece], twin, state)
            old += piece[2] // LANES
            for ahead in follow.get(piece, ()):
                own[ahead] = across(after(sent[ahead], token), ahead[0])
    best = jnp.max(state[4], 1)
    table = jnp.concatenate(
        [
            best[spots[piece] : spots[piece] + piece[2] // LANES]
            for piece in sorted(visits)
        ],
        0,
    ).reshape(chips, group, LANES)
    bit = 1
    while bit < chips:
        split = table.reshape(chips // (2 * bit), 2, bit, group, LANES)
        got = across(split[:, 1], bit)
        table = jnp.stack([split[:, 0], got], 1).reshape(chips, group, LANES)
        bit *= 2
    table = table.reshape(rows // LANES, LANES)
    answer = answer_rows(chip.reshape(1), table, position, inverse, block)
    return answer.reshape(rows)


def solution(mesh):
    in_specs = (P(("parts", "owner"), None), P(("parts", "owner")), P(("parts", "owner")))
    out_specs = P(("parts", "owner"))
    return jax.shard_map(
        on_device, mesh=mesh, in_specs=in_specs, out_specs=out_specs, check_vma=False
    )
```

```python
import functools

import jax
import jax.numpy as jnp
from jax import lax
from jax.experimental import pallas as pl
from jax.experimental.pallas import tpu as pltpu
from jax.sharding import PartitionSpec as P

CL_DEV = 4
CMAX = 2048
EPSILON = 1e-06
MASKED = -30000.0
GROUP = 2 * CL_DEV
LANES = 128
VMEM_LIMIT = 24 * 1024 * 1024
MATCH_LIMIT = 20 * 1024 * 1024


def params():
    return pltpu.CompilerParams(vmem_limit_bytes=VMEM_LIMIT)


def nt_dot(a, b):
    return lax.dot_general(a, b, (((1,), (1,)), ((), ())), preferred_element_type=jnp.float32)


def one_hot(condition):
    return jnp.where(condition, 1.0, 0.0).astype(jnp.bfloat16)


def tile_lanes(x, times):
    return jnp.concatenate([x] * times, 1)


def order_kernel(ids_ref, ranks_ref, pos_ref, keys_ref, local_ref):
    rows = ids_ref.shape[1]
    clusters = local_ref.shape[0]
    chunk = 256
    cluster_iota = lax.broadcasted_iota(jnp.int32, (clusters, chunk), 0)
    before = one_hot(
        lax.broadcasted_iota(jnp.int32, (chunk, chunk), 0)
        < lax.broadcasted_iota(jnp.int32, (chunk, chunk), 1)
    )
    ones = jnp.ones((chunk, LANES), jnp.bfloat16)
    count = jnp.zeros((clusters, LANES), jnp.float32)
    for start in range(0, rows, chunk):
        hot = one_hot(ids_ref[:, start : start + chunk] == cluster_iota)
        prefix = jnp.dot(hot, before, preferred_element_type=jnp.float32)
        local_ref[:, start : start + chunk] = prefix + tile_lanes(count, chunk // LANES)
        count += jnp.dot(hot, ones, preferred_element_type=jnp.float32)
    lower = one_hot(
        lax.broadcasted_iota(jnp.int32, (clusters, clusters), 1)
        < lax.broadcasted_iota(jnp.int32, (clusters, clusters), 0)
    )
    offset = jnp.dot(lower, count.astype(jnp.bfloat16), preferred_element_type=jnp.float32)
    offset = tile_lanes(offset, chunk // LANES)
    high_rows = rows // LANES
    table = jnp.zeros((2 * high_rows, LANES), jnp.float32)
    high_iota = lax.broadcasted_iota(jnp.int32, (high_rows, chunk), 0)
    low_iota = lax.broadcasted_iota(jnp.int32, (LANES, chunk), 0)
    for start in range(0, rows, chunk):
        ids = ids_ref[:, start : start + chunk]
        place = jnp.where(
            ids == cluster_iota, local_ref[:, start : start + chunk] + offset, 0.0
        )
        position = jnp.sum(place, 0, keepdims=True).astype(jnp.int32)
        pos_ref[:, start : start + chunk] = position
        key = (ids & (GROUP - 1)) * CMAX + ranks_ref[:, start : start + chunk]
        high_hot = (position >> 7) == high_iota
        key_high = (key >> 7).astype(jnp.float32)
        key_low = (key & 127).astype(jnp.float32)
        left = jnp.concatenate(
            [jnp.where(high_hot, key_high, 0.0), jnp.where(high_hot, key_low, 0.0)], 0
        ).astype(jnp.bfloat16)
        table += nt_dot(left, one_hot((position & 127) == low_iota))
    keys = (table[:high_rows] * 128.0 + table[high_rows:]).astype(jnp.int32)
    for row in range(high_rows):
        keys_ref[row] = jnp.broadcast_to(keys[row : row + 1], (8, LANES))


def order_rows(ids, ranks, clusters):
    rows = ids.shape[0]
    return pl.pallas_call(
        order_kernel,
        out_shape=(
            jax.ShapeDtypeStruct((1, rows), jnp.int32),
            jax.ShapeDtypeStruct((rows // LANES, 8, LANES), jnp.int32),
        ),
        scratch_shapes=[pltpu.VMEM((clusters, rows), jnp.float32)],
        compiler_params=params(),
        cost_estimate=pl.CostEstimate(flops=10**10, bytes_accessed=10**6, transcendentals=0),
        name="order_rows",
    )(ids.reshape(1, rows), ranks.reshape(1, rows))


def key_rows(keys_ref, row, count, width):
    upper = lax.broadcasted_iota(jnp.int32, (8, LANES), 0) == 0
    tiles = []
    for i in range(count):
        key = keys_ref[row + i]
        tiles.append(jnp.where(upper, key >> 7, key & 127).astype(jnp.float32))
    tiles += [jnp.zeros((8, LANES), jnp.float32)] * (width // LANES - count)
    return jnp.concatenate(tiles, 1).astype(jnp.bfloat16)


def inverse_lanes(x):
    x = x.astype(jnp.float32)
    inverse = lax.rsqrt(jnp.sum(x * x, 1, keepdims=True) + EPSILON)
    return jnp.transpose(jnp.broadcast_to(inverse, (LANES, LANES)))[0:1]


def pick_kernel(counts, norms, start_ref, keys_ref, pos_ref, rows_ref, before_ref, *refs):
    outs = refs[: len(counts)]
    rows, width = rows_ref.shape
    for k, count in enumerate(counts):
        out_ref = outs[k]
        start = start_ref[k]
        tile = min(count, 256)

        def one_tile(i, carry, out_ref=out_ref, start=start, tile=tile):
            target = lax.broadcasted_iota(jnp.int32, (tile, rows), 0) + (start + i * tile)
            picked = jnp.dot(
                one_hot(pos_ref[...] == target), rows_ref[...], preferred_element_type=jnp.float32
            )
            out_ref[pl.ds(pl.multiple_of(i * tile, tile), tile)] = picked.astype(out_ref.dtype)
            return carry

        lax.fori_loop(0, count // tile, one_tile, 0)
        out_ref[count:] = key_rows(keys_ref, start // LANES, count // LANES, width)

    if norms:
        for at in range(0, rows, LANES):
            refs[-1][:, at : at + LANES] = inverse_lanes(rows_ref[at : at + LANES])


def pick_blocks(starts, keys, position, embeddings, before, counts, norms):
    rows, width = embeddings.shape
    vmem = pl.BlockSpec(memory_space=pltpu.VMEM)
    return pl.pallas_call(
        functools.partial(pick_kernel, counts, norms),
        in_specs=[pl.BlockSpec(memory_space=pltpu.SMEM), vmem, vmem, vmem]
        + [pl.BlockSpec(memory_space=pl.ANY)],
        out_shape=tuple(jax.ShapeDtypeStruct((count + 8, width), embeddings.dtype) for count in counts)
        + (jax.ShapeDtypeStruct((1, rows), jnp.float32),) * norms,
        out_specs=(vmem,) * (len(counts) + norms),
        compiler_params=params(),
        cost_estimate=pl.CostEstimate(
            flops=2 * sum(counts) * rows * width, bytes_accessed=4 * rows * width, transcendentals=0
        ),
        name="pick_blocks",
    )(starts, keys, position, embeddings, before)


def new_keys(ref, count):
    parts = ref[count : count + 8, :count].astype(jnp.float32)
    return (parts[0:1] * 128.0 + parts[1:2]).astype(jnp.int32)


def column_best(scores, column_inverse, column_key, query_key):
    count = scores.shape[1]
    rank = query_key & (CMAX - 1)
    base = query_key - rank
    earlier = (tile_lanes(column_key, count // LANES) ^ base) < rank
    scores = jnp.where(earlier, scores * tile_lanes(column_inverse, count // LANES), MASKED)
    return jnp.max(scores.reshape(scores.shape[0] // 8, 8, count), 0)


def row_best(scores, column_inverse, column_key, query_key, best):
    rank = query_key & (CMAX - 1)
    base = query_key - rank
    for start in range(0, scores.shape[1], LANES):
        cut = slice(start, start + LANES)
        earlier = (column_key[:, cut] ^ base) < rank
        best = jnp.maximum(
            best, jnp.where(earlier, scores[:, cut] * column_inverse[:, cut], MASKED)
        )
    return best


def best_of(columns, column_inverse, column_key, queries, query_key):
    return column_best(nt_dot(columns, queries), column_inverse, column_key, query_key)


def joined(ref, first, last):
    return jnp.concatenate([ref[i] for i in range(first, last)], 1)


def flat(x):
    return x.reshape(x.shape[0] * x.shape[1], x.shape[2])


def step_kernel(old, group, own_ref, other_ref, *refs):
    if old:
        rows_ref, inverse_ref, spread_ref, lane_ref, scale_ref, best_in = refs[:6]
        refs = refs[6:]
    rows_out, inverse_out, spread_out, lane_out, scale_out, best_out, token_ref, running, across_best = refs
    fresh = rows_out.shape[0]
    count = fresh * LANES
    full, rest = old // group, old % group
    step = pl.program_id(0)

    @pl.when(step == 0)
    def _():
        for side, ref in ((0, own_ref), (1, other_ref)):
            keys = new_keys(ref, count)
            for slot in range(fresh):
                cut = slice(slot * LANES, (slot + 1) * LANES)
                rows_out[slot, side] = ref[cut]
                x = ref[cut].astype(jnp.float32)
                inverse = lax.rsqrt(jnp.sum(x * x, 1, keepdims=True) + EPSILON)
                inverse_out[slot, side] = jnp.broadcast_to(inverse, (LANES, LANES))
                spread_out[slot, side] = jnp.transpose(
                    jnp.broadcast_to(keys[:, cut], (LANES, LANES))
                )
                if side == 0:
                    lane_out[slot] = jnp.broadcast_to(keys[:, cut], (8, LANES))
                    scale_out[slot] = jnp.transpose(inverse_out[slot, side])[:8]
        running[...] = jnp.full(running.shape, MASKED, jnp.float32)
        across_best[...] = jnp.full(across_best.shape, MASKED, jnp.float32)

    own_key = new_keys(own_ref, count)

    def against_new(queries, query_key, best):
        for slot in range(fresh):
            best = jnp.maximum(
                best,
                best_of(flat(rows_out[slot]), flat(inverse_out[slot]), flat(spread_out[slot]),
                        queries, query_key),
            )
        return best

    def visit(slots):
        old_key = joined(lane_ref, 0, slots)[0:1]
        old_inverse = joined(scale_ref, 0, slots)[0:1]
        queries = flat(rows_ref[:slots, 0])
        old_best = joined(best_in, 0, slots)
        scores = nt_dot(flat(rows_out[:, 0]), queries)
        spread = flat(spread_out[:, 0])
        old_best = jnp.maximum(
            old_best, column_best(scores, flat(inverse_out[:, 0]), spread, old_key)
        )
        across_best[...] = row_best(scores, old_inverse, old_key, spread, across_best[...])
        old_best = jnp.maximum(
            old_best,
            best_of(flat(rows_out[:, 1]), flat(inverse_out[:, 1]), flat(spread_out[:, 1]),
                    queries, old_key),
        )
        for slot in range(slots):
            best_out[slot] = old_best[:, slot * LANES : (slot + 1) * LANES]
        best = jnp.maximum(
            running[...],
            best_of(flat(rows_ref[:slots, 1]), flat(inverse_ref[:slots, 1]),
                    flat(spread_ref[:slots, 1]), own_ref[:count], own_key),
        )
        running[...] = best

    if full:

        @pl.when(step < full)
        def _():
            visit(group)

    @pl.when(step == full)
    def _():
        if rest:
            visit(rest)
        best = against_new(own_ref[:count], own_key, running[...])
        if old:
            turned = [
                jnp.max(
                    jnp.transpose(across_best[slot * LANES : (slot + 1) * LANES]).reshape(
                        LANES // 8, 8, LANES
                    ),
                    0,
                )
                for slot in range(fresh)
            ]
            best = jnp.maximum(best, jnp.concatenate(turned, 1))
        for slot in range(fresh):
            best_out[rest + slot] = best[:, slot * LANES : (slot + 1) * LANES]
        token_ref[...] = best[:, :LANES]


def match_step(old, group, room, own, other, state):
    count, width = own.shape[0] - 8, own.shape[1]
    fresh = count // LANES
    full, rest = old // group, old % group

    def whole(shape):
        return pl.BlockSpec(shape, lambda i: (0,) * len(shape))

    def old_block(shape):
        last = max(-(-old // group) - 1, 0)
        return pl.BlockSpec(
            (group,) + shape, lambda i: (jnp.minimum(i, last),) + (0,) * len(shape)
        )

    def new_block(shape):
        return pl.BlockSpec((fresh,) + shape, lambda i: (old // fresh,) + (0,) * len(shape))

    shapes = ((2, LANES, width), (2, LANES, LANES), (2, LANES, LANES)) + ((8, LANES),) * 3
    dtypes = (own.dtype, jnp.float32, jnp.int32, jnp.int32, jnp.float32, jnp.float32)
    in_specs = [whole(own.shape), whole(own.shape)]
    if old:
        in_specs += [old_block(shape) for shape in shapes]
    return pl.pallas_call(
        functools.partial(step_kernel, old, group),
        grid=(full + 1,),
        in_specs=in_specs,
        out_specs=tuple(new_block(shape) for shape in shapes[:5])
        + (pl.BlockSpec((group, 8, LANES), lambda i: (i, 0, 0)), whole((8, LANES))),
        out_shape=tuple(
            jax.ShapeDtypeStruct((room,) + shape, dtype) for shape, dtype in zip(shapes, dtypes)
        )
        + (jax.ShapeDtypeStruct((8, LANES), jnp.float32),),
        scratch_shapes=[
            pltpu.VMEM((8, count), jnp.float32),
            pltpu.VMEM((count, LANES), jnp.float32),
        ],
        input_output_aliases={2 + i: i for i in range(6)} if old else {},
        compiler_params=pltpu.CompilerParams(vmem_limit_bytes=MATCH_LIMIT),
        cost_estimate=pl.CostEstimate(
            flops=3 * 10**9 if old >= 2 * group else LANES, bytes_accessed=LANES, transcendentals=0
        ),
        name="match_step",
    )(own, other, *state)


def answer_kernel(chip_ref, block_rows, table_ref, pos_ref, inverse_ref, out_ref):
    rows = pos_ref.shape[1]
    chunk = 512
    table = table_ref[...]
    high = table.astype(jnp.bfloat16)
    rest = table - high.astype(jnp.float32)
    middle = rest.astype(jnp.bfloat16)
    low = (rest - middle.astype(jnp.float32)).astype(jnp.bfloat16)
    high_iota = lax.broadcasted_iota(jnp.int32, (rows // LANES, chunk), 0)
    low_iota = lax.broadcasted_iota(jnp.int32, (LANES, chunk), 0)
    for start in range(0, rows, chunk):
        position = pos_ref[:, start : start + chunk] ^ (chip_ref[0] * block_rows)
        hot = one_hot((position >> 7) == high_iota)
        values = sum(
            lax.dot_general(part, hot, (((0,), (0,)), ((), ())), preferred_element_type=jnp.float32)
            for part in (high, middle, low)
        )
        best = jnp.sum(
            jnp.where((position & 127) == low_iota, values, 0.0), 0, keepdims=True
        )
        out_ref[:, start : start + chunk] = jnp.maximum(
            best * inverse_ref[:, start : start + chunk], -1.0
        )


def answer_rows(chip, table, position, inverse, block_rows):
    rows = position.shape[1]

    def body(chip_ref, *refs):
        answer_kernel(chip_ref, block_rows, *refs)

    return pl.pallas_call(
        body,
        in_specs=[pl.BlockSpec(memory_space=pltpu.SMEM)] + [pl.BlockSpec(memory_space=pltpu.VMEM)] * 3,
        out_shape=jax.ShapeDtypeStruct((1, rows), jnp.float32),
        compiler_params=params(),
        name="answer_rows",
    )(chip, table, position, inverse)


def after_kernel(x_ref, token_ref, out_ref):
    pass


def after(x, token):
    return pl.pallas_call(
        after_kernel,
        in_specs=[pl.BlockSpec(memory_space=pl.ANY)] * 2,
        out_specs=pl.BlockSpec(memory_space=pl.ANY),
        out_shape=jax.ShapeDtypeStruct(x.shape, x.dtype),
        input_output_aliases={0: 0},
        compiler_params=pltpu.CompilerParams(vmem_limit_bytes=1024 * 1024),
        cost_estimate=pl.CostEstimate(flops=0, bytes_accessed=0, transcendentals=0),
        name="after",
    )(x, token)


def on_device(embeddings, cluster_ids, member_ranks):
    rows, width = embeddings.shape
    owners = lax.axis_size("owner")
    chips = owners // 2
    block = rows // chips
    group = block // LANES
    room = rows // LANES
    chip = (lax.axis_index("owner") // 2).astype(jnp.int32)

    def across(x, d):
        return lax.ppermute(x, "owner", [(i, i ^ (2 * d)) for i in range(owners)])

    def swap(x):
        return lax.ppermute(x, "owner", [(i, i ^ 1) for i in range(owners)])

    local = (0, 0, block)
    near = [(d, 0, block) for d in range(1, chips // 2)]
    far = [(d, 0, block) for d in range(chips // 2, chips - 1)]
    last = (chips - 1, 0, block)
    rounds = [[local], far[:1], [far[1], *near[:2]]]
    rounds += [list(pair) for pair in zip(near[2:], far[2:])] + [[last]]
    visits = [piece for pieces in rounds for piece in pieces]
    follow = {rounds[turn][-1]: rounds[turn + 2] for turn in range(1, len(rounds) - 2)}
    batches = [rounds[1], [local, *visits[2:]]]

    position, keys = order_rows(cluster_ids, member_ranks, chips * GROUP)
    sent = {}
    for turn, batch in enumerate(batches):
        starts = jnp.stack([(chip ^ d) * block + at for d, at, size in batch])
        counts = [size for d, at, size in batch]
        before = picked[0] if turn else keys
        picked = pick_blocks(
            starts, keys, position, embeddings, before, counts, turn + 1 == len(batches)
        )
        sent.update(zip(batch, picked))
    inverse = picked[-1]
    own = {piece: across(sent[piece], piece[0]) for piece in visits[1:5]}
    own[local] = sent[local]
    state = ()
    old = 0
    spots = {}
    token = None
    for turn, pieces in enumerate(rounds):
        if turn > 1:
            for piece in pieces:
                own[piece] = after(own[piece], token)
        other = [swap(own[piece]) for piece in pieces]
        for piece, twin in zip(pieces, other):
            spots[piece] = old
            *state, token = match_step(old, group, room, own[piece], twin, state)
            old += piece[2] // LANES
            for ahead in follow.get(piece, ()):
                own[ahead] = across(after(sent[ahead], token), ahead[0])
    best = jnp.max(state[5], 1)
    table = jnp.concatenate(
        [
            best[spots[piece] : spots[piece] + piece[2] // LANES]
            for piece in sorted(visits)
        ],
        0,
    ).reshape(chips, group, LANES)
    bit = 1
    while bit < chips:
        split = table.reshape(chips // (2 * bit), 2, bit, group, LANES)
        got = across(split[:, 1], bit)
        table = jnp.stack([split[:, 0], got], 1).reshape(chips, group, LANES)
        bit *= 2
    table = table.reshape(rows // LANES, LANES)
    answer = answer_rows(chip.reshape(1), table, position, inverse, block)
    return answer.reshape(rows)


def solution(mesh):
    in_specs = (P(("parts", "owner"), None), P(("parts", "owner")), P(("parts", "owner")))
    out_specs = P(("parts", "owner"))
    return jax.shard_map(
        on_device, mesh=mesh, in_specs=in_specs, out_specs=out_specs, check_vma=False
    )
```

```python
import functools

import jax
import jax.numpy as jnp
from jax import lax
from jax.experimental import pallas as pl
from jax.experimental.pallas import tpu as pltpu
from jax.sharding import PartitionSpec as P

CL_DEV = 4
CMAX = 2048
EPSILON = 1e-06
MASKED = -30000.0
GROUP = 2 * CL_DEV
LANES = 128
VMEM_LIMIT = 24 * 1024 * 1024
MATCH_LIMIT = 20 * 1024 * 1024


def params():
    return pltpu.CompilerParams(vmem_limit_bytes=VMEM_LIMIT)


def nt_dot(a, b):
    return lax.dot_general(a, b, (((1,), (1,)), ((), ())), preferred_element_type=jnp.float32)


def one_hot(condition):
    return jnp.where(condition, 1.0, 0.0).astype(jnp.bfloat16)


def tile_lanes(x, times):
    return jnp.concatenate([x] * times, 1)


def order_kernel(ids_ref, ranks_ref, pos_ref, keys_ref, local_ref):
    rows = ids_ref.shape[1]
    clusters = local_ref.shape[0]
    chunk = 256
    cluster_iota = lax.broadcasted_iota(jnp.int32, (clusters, chunk), 0)
    before = one_hot(
        lax.broadcasted_iota(jnp.int32, (chunk, chunk), 0)
        < lax.broadcasted_iota(jnp.int32, (chunk, chunk), 1)
    )
    ones = jnp.ones((chunk, LANES), jnp.bfloat16)
    count = jnp.zeros((clusters, LANES), jnp.float32)
    for start in range(0, rows, chunk):
        hot = one_hot(ids_ref[:, start : start + chunk] == cluster_iota)
        prefix = jnp.dot(hot, before, preferred_element_type=jnp.float32)
        local_ref[:, start : start + chunk] = prefix + tile_lanes(count, chunk // LANES)
        count += jnp.dot(hot, ones, preferred_element_type=jnp.float32)
    lower = one_hot(
        lax.broadcasted_iota(jnp.int32, (clusters, clusters), 1)
        < lax.broadcasted_iota(jnp.int32, (clusters, clusters), 0)
    )
    offset = jnp.dot(lower, count.astype(jnp.bfloat16), preferred_element_type=jnp.float32)
    offset = tile_lanes(offset, chunk // LANES)
    high_rows = rows // LANES
    table = jnp.zeros((2 * high_rows, LANES), jnp.float32)
    high_iota = lax.broadcasted_iota(jnp.int32, (high_rows, chunk), 0)
    low_iota = lax.broadcasted_iota(jnp.int32, (LANES, chunk), 0)
    for start in range(0, rows, chunk):
        ids = ids_ref[:, start : start + chunk]
        place = jnp.where(
            ids == cluster_iota, local_ref[:, start : start + chunk] + offset, 0.0
        )
        position = jnp.sum(place, 0, keepdims=True).astype(jnp.int32)
        pos_ref[:, start : start + chunk] = position
        key = (ids & (GROUP - 1)) * CMAX + ranks_ref[:, start : start + chunk]
        high_hot = (position >> 7) == high_iota
        key_high = (key >> 7).astype(jnp.float32)
        key_low = (key & 127).astype(jnp.float32)
        left = jnp.concatenate(
            [jnp.where(high_hot, key_high, 0.0), jnp.where(high_hot, key_low, 0.0)], 0
        ).astype(jnp.bfloat16)
        table += nt_dot(left, one_hot((position & 127) == low_iota))
    keys = (table[:high_rows] * 128.0 + table[high_rows:]).astype(jnp.int32)
    for row in range(high_rows):
        keys_ref[row] = jnp.broadcast_to(keys[row : row + 1], (8, LANES))


def order_rows(ids, ranks, clusters):
    rows = ids.shape[0]
    return pl.pallas_call(
        order_kernel,
        out_shape=(
            jax.ShapeDtypeStruct((1, rows), jnp.int32),
            jax.ShapeDtypeStruct((rows // LANES, 8, LANES), jnp.int32),
        ),
        scratch_shapes=[pltpu.VMEM((clusters, rows), jnp.float32)],
        compiler_params=params(),
        cost_estimate=pl.CostEstimate(flops=10**10, bytes_accessed=10**6, transcendentals=0),
        name="order_rows",
    )(ids.reshape(1, rows), ranks.reshape(1, rows))


def key_rows(keys_ref, row, count, width):
    upper = lax.broadcasted_iota(jnp.int32, (8, LANES), 0) == 0
    tiles = []
    for i in range(count):
        key = keys_ref[row + i]
        tiles.append(jnp.where(upper, key >> 7, key & 127).astype(jnp.float32))
    tiles += [jnp.zeros((8, LANES), jnp.float32)] * (width // LANES - count)
    return jnp.concatenate(tiles, 1).astype(jnp.bfloat16)


def inverse_lanes(x):
    x = x.astype(jnp.float32)
    inverse = lax.rsqrt(jnp.sum(x * x, 1, keepdims=True) + EPSILON)
    return jnp.transpose(jnp.broadcast_to(inverse, (LANES, LANES)))[0:1]


def pick_kernel(counts, norms, start_ref, keys_ref, pos_ref, rows_ref, before_ref, *refs):
    outs = refs[: len(counts)]
    rows, width = rows_ref.shape
    for k, count in enumerate(counts):
        out_ref = outs[k]
        start = start_ref[k]
        tile = min(count, 256)

        def one_tile(i, carry, out_ref=out_ref, start=start, tile=tile):
            target = lax.broadcasted_iota(jnp.int32, (tile, rows), 0) + (start + i * tile)
            picked = jnp.dot(
                one_hot(pos_ref[...] == target), rows_ref[...], preferred_element_type=jnp.float32
            )
            out_ref[pl.ds(pl.multiple_of(i * tile, tile), tile)] = picked.astype(out_ref.dtype)
            return carry

        lax.fori_loop(0, count // tile, one_tile, 0)
        out_ref[count:] = key_rows(keys_ref, start // LANES, count // LANES, width)

    if norms:
        for at in range(0, rows, LANES):
            refs[-1][:, at : at + LANES] = inverse_lanes(rows_ref[at : at + LANES])


def pick_blocks(starts, keys, position, embeddings, before, counts, norms):
    rows, width = embeddings.shape
    vmem = pl.BlockSpec(memory_space=pltpu.VMEM)
    return pl.pallas_call(
        functools.partial(pick_kernel, counts, norms),
        in_specs=[pl.BlockSpec(memory_space=pltpu.SMEM), vmem, vmem, vmem]
        + [pl.BlockSpec(memory_space=pl.ANY)],
        out_shape=tuple(jax.ShapeDtypeStruct((count + 8, width), embeddings.dtype) for count in counts)
        + (jax.ShapeDtypeStruct((1, rows), jnp.float32),) * norms,
        out_specs=(vmem,) * (len(counts) + norms),
        compiler_params=params(),
        cost_estimate=pl.CostEstimate(
            flops=2 * sum(counts) * rows * width, bytes_accessed=4 * rows * width, transcendentals=0
        ),
        name="pick_blocks",
    )(starts, keys, position, embeddings, before)


def new_keys(ref, count):
    parts = ref[count : count + 8, :count].astype(jnp.float32)
    return (parts[0:1] * 128.0 + parts[1:2]).astype(jnp.int32)


def column_best(scores, column_inverse, column_key, query_key):
    count = scores.shape[1]
    rank = query_key & (CMAX - 1)
    base = query_key - rank
    earlier = (tile_lanes(column_key, count // LANES) ^ base) < rank
    scores = jnp.where(earlier, scores * tile_lanes(column_inverse, count // LANES), MASKED)
    return jnp.max(scores.reshape(scores.shape[0] // 8, 8, count), 0)


def row_best(scores, column_inverse, column_key, query_key, best):
    rank = query_key & (CMAX - 1)
    base = query_key - rank
    for start in range(0, scores.shape[1], LANES):
        cut = slice(start, start + LANES)
        earlier = (column_key[:, cut] ^ base) < rank
        best = jnp.maximum(
            best, jnp.where(earlier, scores[:, cut] * column_inverse[:, cut], MASKED)
        )
    return best


def best_of(columns, column_inverse, column_key, queries, query_key):
    return column_best(nt_dot(columns, queries), column_inverse, column_key, query_key)


def joined(ref, first, last):
    return jnp.concatenate([ref[i] for i in range(first, last)], 1)


def flat(x):
    return x.reshape(x.shape[0] * x.shape[1], x.shape[2])


def step_kernel(old, group, own_ref, other_ref, *refs):
    if old:
        rows_ref, inverse_ref, spread_ref, lane_ref, scale_ref, best_in = refs[:6]
        refs = refs[6:]
    rows_out, inverse_out, spread_out, lane_out, scale_out, best_out, token_ref, running, across_best = refs
    fresh = rows_out.shape[0]
    count = fresh * LANES
    full, rest = old // group, old % group
    step = pl.program_id(0)

    @pl.when(step == 0)
    def _():
        for side, ref in ((0, own_ref), (1, other_ref)):
            keys = new_keys(ref, count)
            for slot in range(fresh):
                cut = slice(slot * LANES, (slot + 1) * LANES)
                rows_out[slot, side] = ref[cut]
                x = ref[cut].astype(jnp.float32)
                inverse = lax.rsqrt(jnp.sum(x * x, 1, keepdims=True) + EPSILON)
                inverse_out[slot, side] = jnp.broadcast_to(inverse, (LANES, LANES))
                spread_out[slot, side] = jnp.transpose(
                    jnp.broadcast_to(keys[:, cut], (LANES, LANES))
                )
                if side == 0:
                    lane_out[slot] = jnp.broadcast_to(keys[:, cut], (8, LANES))
                    scale_out[slot] = jnp.transpose(inverse_out[slot, side])[:8]
        running[...] = jnp.full(running.shape, MASKED, jnp.float32)
        across_best[...] = jnp.full(across_best.shape, MASKED, jnp.float32)

    own_key = new_keys(own_ref, count)

    def against_new(queries, query_key, best):
        for slot in range(fresh):
            best = jnp.maximum(
                best,
                best_of(flat(rows_out[slot]), flat(inverse_out[slot]), flat(spread_out[slot]),
                        queries, query_key),
            )
        return best

    def visit(slots):
        old_key = joined(lane_ref, 0, slots)[0:1]
        old_inverse = joined(scale_ref, 0, slots)[0:1]
        queries = flat(rows_ref[:slots, 0])
        old_best = joined(best_in, 0, slots)
        scores = nt_dot(flat(rows_out[:, 0]), queries)
        spread = flat(spread_out[:, 0])
        old_best = jnp.maximum(
            old_best, column_best(scores, flat(inverse_out[:, 0]), spread, old_key)
        )
        across_best[...] = row_best(scores, old_inverse, old_key, spread, across_best[...])
        old_best = jnp.maximum(
            old_best,
            best_of(flat(rows_out[:, 1]), flat(inverse_out[:, 1]), flat(spread_out[:, 1]),
                    queries, old_key),
        )
        for slot in range(slots):
            best_out[slot] = old_best[:, slot * LANES : (slot + 1) * LANES]
        best = jnp.maximum(
            running[...],
            best_of(flat(rows_ref[:slots, 1]), flat(inverse_ref[:slots, 1]),
                    flat(spread_ref[:slots, 1]), own_ref[:count], own_key),
        )
        running[...] = best

    if full:

        @pl.when(step < full)
        def _():
            visit(group)

    @pl.when(step == full)
    def _():
        if rest:
            visit(rest)
        best = against_new(own_ref[:count], own_key, running[...])
        if old:
            turned = [
                jnp.max(
                    jnp.transpose(across_best[slot * LANES : (slot + 1) * LANES]).reshape(
                        LANES // 8, 8, LANES
                    ),
                    0,
                )
                for slot in range(fresh)
            ]
            best = jnp.maximum(best, jnp.concatenate(turned, 1))
        for slot in range(fresh):
            best_out[rest + slot] = best[:, slot * LANES : (slot + 1) * LANES]
        token_ref[...] = best[:, :LANES]


def match_step(old, group, room, own, other, state):
    count, width = own.shape[0] - 8, own.shape[1]
    fresh = count // LANES
    full, rest = old // group, old % group

    def whole(shape):
        return pl.BlockSpec(shape, lambda i: (0,) * len(shape))

    def old_block(shape):
        last = max(-(-old // group) - 1, 0)
        return pl.BlockSpec(
            (group,) + shape, lambda i: (jnp.minimum(i, last),) + (0,) * len(shape)
        )

    def new_block(shape):
        return pl.BlockSpec((fresh,) + shape, lambda i: (old // fresh,) + (0,) * len(shape))

    shapes = ((2, LANES, width), (2, LANES, LANES), (2, LANES, LANES)) + ((8, LANES),) * 3
    dtypes = (own.dtype, jnp.float32, jnp.int32, jnp.int32, jnp.float32, jnp.float32)
    in_specs = [whole(own.shape), whole(own.shape)]
    if old:
        in_specs += [old_block(shape) for shape in shapes]
    return pl.pallas_call(
        functools.partial(step_kernel, old, group),
        grid=(full + 1,),
        in_specs=in_specs,
        out_specs=tuple(new_block(shape) for shape in shapes[:5])
        + (pl.BlockSpec((group, 8, LANES), lambda i: (i, 0, 0)), whole((8, LANES))),
        out_shape=tuple(
            jax.ShapeDtypeStruct((room,) + shape, dtype) for shape, dtype in zip(shapes, dtypes)
        )
        + (jax.ShapeDtypeStruct((8, LANES), jnp.float32),),
        scratch_shapes=[
            pltpu.VMEM((8, count), jnp.float32),
            pltpu.VMEM((count, LANES), jnp.float32),
        ],
        input_output_aliases={2 + i: i for i in range(6)} if old else {},
        compiler_params=pltpu.CompilerParams(vmem_limit_bytes=MATCH_LIMIT),
        cost_estimate=pl.CostEstimate(
            flops=3 * 10**9 if old >= 2 * group else LANES, bytes_accessed=LANES, transcendentals=0
        ),
        name="match_step",
    )(own, other, *state)


def answer_kernel(chip_ref, block_rows, table_ref, pos_ref, inverse_ref, out_ref):
    rows = pos_ref.shape[1]
    chunk = 512
    table = table_ref[...]
    high = table.astype(jnp.bfloat16)
    rest = table - high.astype(jnp.float32)
    middle = rest.astype(jnp.bfloat16)
    low = (rest - middle.astype(jnp.float32)).astype(jnp.bfloat16)
    high_iota = lax.broadcasted_iota(jnp.int32, (rows // LANES, chunk), 0)
    low_iota = lax.broadcasted_iota(jnp.int32, (LANES, chunk), 0)
    for start in range(0, rows, chunk):
        position = pos_ref[:, start : start + chunk] ^ (chip_ref[0] * block_rows)
        hot = one_hot((position >> 7) == high_iota)
        values = sum(
            lax.dot_general(part, hot, (((0,), (0,)), ((), ())), preferred_element_type=jnp.float32)
            for part in (high, middle, low)
        )
        best = jnp.sum(
            jnp.where((position & 127) == low_iota, values, 0.0), 0, keepdims=True
        )
        out_ref[:, start : start + chunk] = jnp.maximum(
            best * inverse_ref[:, start : start + chunk], -1.0
        )


def answer_rows(chip, table, position, inverse, block_rows):
    rows = position.shape[1]

    def body(chip_ref, *refs):
        answer_kernel(chip_ref, block_rows, *refs)

    return pl.pallas_call(
        body,
        in_specs=[pl.BlockSpec(memory_space=pltpu.SMEM)] + [pl.BlockSpec(memory_space=pltpu.VMEM)] * 3,
        out_shape=jax.ShapeDtypeStruct((1, rows), jnp.float32),
        compiler_params=params(),
        name="answer_rows",
    )(chip, table, position, inverse)


def after_kernel(x_ref, token_ref, out_ref):
    pass


def after(x, token):
    return pl.pallas_call(
        after_kernel,
        in_specs=[pl.BlockSpec(memory_space=pl.ANY)] * 2,
        out_specs=pl.BlockSpec(memory_space=pl.ANY),
        out_shape=jax.ShapeDtypeStruct(x.shape, x.dtype),
        input_output_aliases={0: 0},
        compiler_params=pltpu.CompilerParams(vmem_limit_bytes=1024 * 1024),
        cost_estimate=pl.CostEstimate(flops=0, bytes_accessed=0, transcendentals=0),
        name="after",
    )(x, token)


def on_device(embeddings, cluster_ids, member_ranks):
    rows, width = embeddings.shape
    owners = lax.axis_size("owner")
    chips = owners // 2
    block = rows // chips
    group = block // LANES
    room = rows // LANES
    chip = (lax.axis_index("owner") // 2).astype(jnp.int32)

    def across(x, d):
        return lax.ppermute(x, "owner", [(i, i ^ (2 * d)) for i in range(owners)])

    def swap(x):
        return lax.ppermute(x, "owner", [(i, i ^ 1) for i in range(owners)])

    local = (0, 0, block)
    near = [(d, 0, block) for d in range(1, chips // 2)]
    far = [(d, 0, block) for d in range(chips // 2, chips - 1)]
    last = (chips - 1, 0, block)
    rounds = [[local], far[:1], [far[1], *near[:2]]]
    rounds += [list(pair) for pair in zip(near[2:], far[2:])] + [[last]]
    visits = [piece for pieces in rounds for piece in pieces]
    follow = {rounds[turn][-1]: rounds[turn + 2] for turn in range(1, len(rounds) - 2)}
    batches = [rounds[1], [local, *visits[2:]]]

    position, keys = order_rows(cluster_ids, member_ranks, chips * GROUP)
    sent = {}
    for turn, batch in enumerate(batches):
        starts = jnp.stack([(chip ^ d) * block + at for d, at, size in batch])
        counts = [size for d, at, size in batch]
        before = picked[0] if turn else keys
        picked = pick_blocks(
            starts, keys, position, embeddings, before, counts, turn + 1 == len(batches)
        )
        sent.update(zip(batch, picked))
    inverse = picked[-1]
    own = {piece: across(sent[piece], piece[0]) for piece in visits[1:5]}
    own[local] = sent[local]
    state = ()
    old = 0
    spots = {}
    token = None
    for turn, pieces in enumerate(rounds):
        if turn > 1:
            for piece in pieces:
                own[piece] = after(own[piece], token)
        other = [swap(own[piece]) for piece in pieces]
        for piece, twin in zip(pieces, other):
            spots[piece] = old
            *state, token = match_step(old, group, room, own[piece], twin, state)
            old += piece[2] // LANES
            for ahead in follow.get(piece, ()):
                own[ahead] = across(after(sent[ahead], token), ahead[0])
    best = jnp.max(state[5], 1)
    table = jnp.concatenate(
        [
            best[spots[piece] : spots[piece] + piece[2] // LANES]
            for piece in sorted(visits)
        ],
        0,
    ).reshape(chips, group, LANES)
    bit = chips // 2
    while bit:
        split = table.reshape(chips // (2 * bit), 2, bit, group, LANES)
        got = across(split[:, 1], bit)
        table = jnp.stack([split[:, 0], got], 1).reshape(chips, group, LANES)
        bit //= 2
    table = table.reshape(rows // LANES, LANES)
    answer = answer_rows(chip.reshape(1), table, position, inverse, block)
    return answer.reshape(rows)


def solution(mesh):
    in_specs = (P(("parts", "owner"), None), P(("parts", "owner")), P(("parts", "owner")))
    out_specs = P(("parts", "owner"))
    return jax.shard_map(
        on_device, mesh=mesh, in_specs=in_specs, out_specs=out_specs, check_vma=False
    )
```
